128 devices in a mesh: rep: 16 (over x, z), tp: 8 (over y, core).
Axes of the slice: x: 4, y: 4, z: 4, core: 2. Of those that a mesh axis runs over, the one named last changes fastest.
Arguments:
- tokens: bfloat16 [768, 16384], P(None, ('rep', 'tp')), may hold values from -6 to 6
- gate_weight: bfloat16 [16384, 26624], P(('rep', 'tp')), may hold values from -1 to 1
- up_weight: bfloat16 [16384, 26624], P(('rep', 'tp')), may hold values from -1 to 1
- down_weight: bfloat16 [26624, 16384], P(None, ('rep', 'tp')), may hold values from -1 to 1
Outputs:
- output_block: bfloat16 [768, 16384], P(None, ('rep', 'tp'))
- peak_values: float32 [3], replicated
The draws below stay inside these ranges and needn't reach their ends.
All inputs are finite; a program needn't handle non-finite values. Where the reference program divides by a largest or mean magnitude, that divisor is 1e-20 or more.
Results may differ from the reference program's by a relative error of at most 0.0051.
Values may be sent and summed in bfloat16 or wider, within the bound.
A program may use at most 192 MiB of HBM per device.

```python
import math
import jax
import jax.numpy as jnp

D = 16384
FF = 26624
TOK = 768


def spread_weight(key, values, ramp_axis, fan_in, top):
    row_count, col_count = values.shape
    row_key, col_key = jax.random.split(key)
    row_scale = jnp.exp(jax.random.uniform(row_key, (row_count, 1), jnp.float32) * math.log(3.4))
    col_scale = jnp.exp(jax.random.uniform(col_key, (1, col_count), jnp.float32) * math.log(3.0))
    length = values.shape[ramp_axis]
    position = jnp.arange(length, dtype=jnp.float32) / max(length - 1, 1)
    rising = jnp.power(jnp.float32(top), position)
    rising = rising[:, None] if ramp_axis == 0 else rising[None, :]
    spread = values * row_scale * col_scale * rising / (7.0 * math.sqrt(fan_in))
    return jnp.clip(spread, -1.0, 1.0).astype(jnp.bfloat16)


def draw_gate_weight(key, part):
    key = jax.random.fold_in(key, 11)
    base_key, scale_key = jax.random.split(key)
    values = jax.random.normal(base_key, (D, FF), jnp.float32)
    return spread_weight(scale_key, values, 0, D, 3.0)


def draw_up_weight(key, part):
    key = jax.random.fold_in(key, 23)
    base_key, scale_key = jax.random.split(key)
    values = jax.random.normal(base_key, (D, FF), jnp.float32)
    return spread_weight(scale_key, values, 0, D, 3.0)


def draw_down_weight(key, part):
    key = jax.random.fold_in(key, 37)
    base_key, scale_key = jax.random.split(key)
    values = jax.random.normal(base_key, (FF, D), jnp.float32)
    return spread_weight(scale_key, values, 1, FF, 3.0)


def level_of(rng, dims, pieces, smallest, largest):
    factor_of = 1.0
    for dim, blocks in pieces:
        draws = jax.random.uniform(jax.random.fold_in(jax.random.fold_in(rng, 6), dim), (blocks,), jnp.float32, smallest / len(pieces), largest / len(pieces))
        factor_of = factor_of * jnp.repeat(jnp.exp(draws), dims[dim] // blocks).reshape((-1,) + (1,) * (len(dims) - 1 - dim))
    return factor_of


def gaussian(stream_key, shape, width, reach, pieces=(), kind=jnp.bfloat16):
    drawn = width * jax.random.normal(stream_key, shape, jnp.float32)
    if pieces:
        drawn = drawn * level_of(stream_key, shape, pieces, -0.22, 0.18)
    return jnp.clip(drawn, -reach, reach).astype(kind)


def setup_inputs(seed: int = 0) -> dict:
    key_list = jax.random.split(jax.random.key(seed), 5)
    return {
        "tokens": gaussian(key_list[0], (TOK, D), 1.0, 6.0, ((1, 128),)),
        "gate_weight": draw_gate_weight(jax.random.fold_in(key_list[4], 71), 0),
        "up_weight": draw_up_weight(jax.random.fold_in(key_list[4], 71), 0),
        "down_weight": draw_down_weight(jax.random.fold_in(key_list[4], 71), 0),
    }


def quantize(weight):
    wide = weight.astype(jnp.float32)
    peak_value = jnp.max(jnp.abs(wide))
    factor = 127.0 / peak_value
    scaled = jnp.floor(wide * factor + 0.5).astype(jnp.bfloat16)
    return scaled, peak_value


def reference(tokens, gate_weight, up_weight, down_weight):
    gate_scaled, gate_peak = quantize(gate_weight)
    gate_sum = jnp.dot(tokens, gate_scaled, preferred_element_type=jnp.float32) * (gate_peak / 127.0)
    up_scaled, up_peak = quantize(up_weight)
    up_sum = jnp.dot(tokens, up_scaled, preferred_element_type=jnp.float32) * (up_peak / 127.0)
    hidden = (jax.nn.silu(gate_sum) * up_sum).astype(jnp.bfloat16)
    down_scaled, down_peak = quantize(down_weight)
    output_block = (jnp.dot(hidden, down_scaled, preferred_element_type=jnp.float32) * (down_peak / 127.0)).astype(jnp.bfloat16)
    return output_block, jnp.stack([gate_peak, up_peak, down_peak])
```

```python
import functools

import jax
import jax.numpy as jnp
from jax import lax
from jax.experimental import pallas as pl
from jax.experimental.pallas import tpu as pltpu
from jax.sharding import PartitionSpec as P

MESH = pl.DeviceIdType.MESH
SIDE = 4
SUM_AXES = ((1, 2), (2, 0), (0, 1))


def class_widths(ff):
    units = ff // (8 * 128)
    first = (units + 2) // 3
    second = (units - first + 1) // 2
    return [first * 128, second * 128, (units - first - second) * 128]


def class_bases(widths):
    return [0, 8 * widths[0], 8 * (widths[0] + widths[1])]


def place():
    rep = lax.axis_index("rep")
    tp = lax.axis_index("tp")
    return (rep // SIDE, tp // 2, lax.rem(rep, SIDE)), lax.rem(tp, 2)


def device_at(xyz, core):
    return (xyz[0] * SIDE + xyz[2], xyz[1] * 2 + core)


def moved(xyz, axis, step):
    out = list(xyz)
    out[axis] = lax.rem(xyz[axis] + step, SIDE)
    return tuple(out)


def mult(value, of):
    return pl.multiple_of(value, of)


class Mail:
    def __init__(self, send_sems, recv_sems):
        self.send_sems, self.recv_sems, self.used, self.sent = send_sems, recv_sems, 0, []

    def post(self, src, dst, device):
        copy = pltpu.make_async_remote_copy(
            src_ref=src,
            dst_ref=dst,
            send_sem=self.send_sems.at[self.used],
            recv_sem=self.recv_sems.at[self.used],
            device_id=device,
            device_id_type=MESH,
        )
        self.used += 1
        copy.start()
        self.sent.append(copy)
        return copy

    def finish(self):
        for copy in self.sent:
            copy.wait_send()


def greet(partners):
    barrier = pltpu.get_barrier_semaphore()
    for partner in partners:
        pl.semaphore_signal(barrier, inc=1, device_id=partner, device_id_type=MESH)
    pl.semaphore_wait(barrier, len(partners))


def scale_rows(ref, rows, columns, factor, step=32):
    def body(i, carry):
        at = pl.ds(mult(i * step, step), step)
        wide = ref[at, :].astype(jnp.float32)
        ref[at, :] = jnp.floor(wide * factor + 0.5).astype(jnp.bfloat16)
        return carry

    lax.fori_loop(0, rows // step, body, 0)


def kernel_in(widths, bases, tokens, gate, up, down, *refs):
    refs = list(refs)

    def take(n):
        out = refs[:n]
        del refs[:n]
        return out

    hidden_out = take(3)
    (peaks_out,) = take(1)
    down_land = take(3)
    gate_w, up_w, tok, part, near, total, far = (take(3) for _ in range(7))
    acc, peak_send, peak_recv, send_sems, recv_sems, own_sems, load_sems = take(7)
    toks, feat = tokens.shape
    quarter, slab = toks // 4, toks // 16
    xyz, core = place()
    other = 1 - core

    partners = [device_at(xyz, other)]
    for axis in range(3):
        for step in range(1, SIDE):
            for c in range(2):
                partners.append(device_at(moved(xyz, axis, step), c))
    greet(partners)

    mail = Mail(send_sems, recv_sems)
    own = []

    def spread(kind):
        arrivals = [[], [], []]
        for step in range(SIDE):
            for flip in range(2):
                if step == 0 and flip == 0:
                    continue
                for g in range(3):
                    there = moved(xyz, g, step)
                    peer_core = core if flip == 0 else other
                    slot = mult((xyz[g] * 2 + core) * feat, feat)
                    part_no = there[g] * 2 + peer_core
                    if kind == 2:
                        src, dst = tokens, tok[g].at[:, pl.ds(slot, feat)]
                    else:
                        col = mult(bases[g] + part_no * widths[g], 128)
                        src = (gate, up)[kind].at[:, pl.ds(col, widths[g])]
                        dst = (gate_w, up_w)[kind][g].at[pl.ds(slot, feat), :]
                    arrivals[g].append(mail.post(src, dst, device_at(there, peer_core)))
        for g in range(3):
            slot = mult((xyz[g] * 2 + core) * feat, feat)
            if kind == 2:
                src, dst = tokens, tok[g].at[:, pl.ds(slot, feat)]
            else:
                col = mult(bases[g] + (xyz[g] * 2 + core) * widths[g], 128)
                src = (gate, up)[kind].at[:, pl.ds(col, widths[g])]
                dst = (gate_w, up_w)[kind][g].at[pl.ds(slot, feat), :]
            copy = pltpu.make_async_copy(src, dst, own_sems.at[kind * 3 + g])
            copy.start()
            own.append(copy)
        return arrivals

    gate_in = spread(0)
    tok_in = spread(2)
    up_in = spread(1)

    def peak_of(load, wave):
        slots = load(wave)
        best = None
        for view in slots:
            rows, cols = view.shape

            def body(i, carry, view=view):
                return jnp.maximum(carry, jnp.abs(view[pl.ds(mult(i * 16, 16), 16), :]))

            top = lax.fori_loop(0, rows // 16, body, jnp.zeros((16, cols), jnp.bfloat16))
            top = jnp.max(top.astype(jnp.float32))
            best = top if best is None else jnp.maximum(best, top)
        return best

    def load_rows(source):
        def run(wave):
            views, copies = [], []
            total_cols = source.shape[1]
            at = 0
            for g in range(3):
                for k in range(2):
                    for r in range(toks // feat):
                        width = min(widths[g], total_cols - at)
                        if width <= 0:
                            continue
                        view = part[g].at[k, pl.ds(r * feat, feat), pl.ds(0, width)]
                        copies.append(
                            pltpu.make_async_copy(
                                source.at[:, pl.ds(at, width)], view, load_sems.at[len(views)]
                            )
                        )
                        views.append(view)
                        at += width
            for copy in copies:
                copy.start()
            for copy in copies:
                copy.wait()
            return views

        return run

    def load_columns(source):
        def run(wave):
            views, copies = [], []
            total_rows = source.shape[0]
            at = 0
            for g in range(3):
                for k in range(2):
                    for j in range(widths[g] // feat):
                        height = min(toks, total_rows - at)
                        if height <= 0:
                            continue
                        view = part[g].at[k, pl.ds(0, height), pl.ds(j * feat, feat)]
                        copies.append(
                            pltpu.make_async_copy(
                                source.at[pl.ds(at, height), :], view, load_sems.at[len(views)]
                            )
                        )
                        views.append(view)
                        at += height
            for copy in copies:
                copy.start()
            for copy in copies:
                copy.wait()
            return views

        return run

    tops = [
        peak_of(load_rows(gate), 0),
        peak_of(load_rows(up), 1),
        peak_of(load_columns(down), 2),
    ]
    row = lax.broadcasted_iota(jnp.int32, (8, 128), 0)
    tile = jnp.where(row == 0, tops[0], jnp.where(row == 1, tops[1], tops[2]))
    got = 0
    for axis in range(3):
        peak_send[axis] = tile
        waits = []
        for step in range(SIDE):
            for flip in range(2):
                if step == 0 and flip == 0 or axis > 0 and flip == 1:
                    continue
                there = device_at(moved(xyz, axis, step), core if flip == 0 else other)
                waits.append(mail.post(peak_send.at[axis], peak_recv.at[got], there))
                got += 1
        for back, copy in enumerate(waits):
            copy.wait_recv()
            tile = jnp.maximum(tile, peak_recv[got - len(waits) + back])
    peaks_out[...] = tile
    peaks = [jnp.max(tile[k : k + 1, :]) for k in range(3)]
    factors = [jnp.max(127.0 / tile[k : k + 1, :]) for k in range(3)]
    units = [jnp.max(tile[k : k + 1, :] / 127.0) for k in range(3)]

    def partial_sums(kind, g, weights):
        width = widths[g]
        cols = 384 if width % 384 == 0 else 256 if width % 256 == 0 else 128
        b = xyz[SUM_AXES[g][0]]

        def body(j, carry):
            at = pl.ds(mult(j * cols, 128), cols)
            acc[:, pl.ds(0, cols)] = jnp.dot(
                tok[g][...], weights[:, at], preferred_element_type=jnp.float32
            )
            part[g][kind, :, at] = acc[:, pl.ds(0, cols)].astype(jnp.bfloat16)
            mine = pl.ds(mult(b * quarter, quarter), quarter)
            total[g][kind, :, at] = acc[mine, pl.ds(0, cols)]
            return carry

        lax.fori_loop(0, width // cols, body, 0)

    near_in = [[], [], []]

    def send_near(kind, g):
        axis = SUM_AXES[g][0]
        for step in (2, 1, 3):
            there = moved(xyz, axis, step)
            rows = pl.ds(mult(there[axis] * quarter, quarter), quarter)
            near_in[g].append(
                mail.post(
                    part[g].at[kind, rows, :],
                    near[g].at[kind, step - 1],
                    device_at(there, core),
                )
            )

    down_in = []

    def spread_down():
        for step in (2, 1, 3):
            for g in range(3):
                there = moved(xyz, g, step)
                start = mult(bases[g] + there[g] * 2 * widths[g], 128)
                down_in.append(
                    mail.post(
                        down.at[pl.ds(start, 2 * widths[g]), :],
                        down_land[g].at[:, pl.ds(mult(xyz[g] * feat, feat), feat)],
                        device_at(there, core),
                    )
                )
        for g in range(3):
            start = mult(bases[g] + xyz[g] * 2 * widths[g], 128)
            copy = pltpu.make_async_copy(
                down.at[pl.ds(start, 2 * widths[g]), :],
                down_land[g].at[:, pl.ds(mult(xyz[g] * feat, feat), feat)],
                own_sems.at[9 + g],
            )
            copy.start()
            own.append(copy)

    for kind, (weights, arrivals) in enumerate(((gate_w, gate_in), (up_w, up_in))):
        for g in range(3):
            for copy in arrivals[g]:
                copy.wait_recv()
            own[kind * 6 + g].wait()
            scale_rows(weights[g], 8 * feat, widths[g], factors[kind])
            if kind == 0:
                for copy in tok_in[g]:
                    copy.wait_recv()
                own[3 + g].wait()
            partial_sums(kind, g, weights[g])
            send_near(kind, g)
            if kind == 1 and g == 0:
                spread_down()

    far_in = [[], [], []]
    for g in range(3):
        axis = SUM_AXES[g][1]
        for copy in near_in[g]:
            copy.wait_recv()
        for kind in range(2):

            def body(i, carry, kind=kind, g=g):
                at = pl.ds(mult(i * 16, 16), 16)
                terms = [near[g][kind, n, at, :].astype(jnp.float32) for n in range(3)]
                total[g][kind, at, :] = (total[g][kind, at, :] + terms[1]) + (terms[0] + terms[2])
                return carry

            lax.fori_loop(0, quarter // 16, body, 0)
            for step in (2, 1, 3):
                there = moved(xyz, axis, step)
                rows = pl.ds(mult(there[axis] * slab, slab), slab)
                far_in[g].append(
                    mail.post(
                        total[g].at[kind, rows, :],
                        far[g].at[kind, step - 1],
                        device_at(there, core),
                    )
                )
    for g in range(3):
        axis = SUM_AXES[g][1]
        for copy in far_in[g]:
            copy.wait_recv()

        def body(i, carry, g=g, axis=axis):
            at = pl.ds(mult(i * 16, 16), 16)
            mine = pl.ds(mult(xyz[axis] * slab + i * 16, 16), 16)
            sums = []
            for kind in range(2):
                value = (total[g][kind, mine, :] + far[g][kind, 1, at, :]) + (
                    far[g][kind, 0, at, :] + far[g][kind, 2, at, :]
                )
                sums.append(value * units[kind])
            hidden = sums[0] / (1.0 + jnp.exp(-sums[0])) * sums[1]
            hidden_out[g][at, :] = hidden.astype(jnp.bfloat16)
            return carry

        lax.fori_loop(0, slab // 16, body, 0)
    for copy in down_in:
        copy.wait_recv()
    for copy in own[9:]:
        copy.wait()
    mail.finish()


def kernel_out(widths, *refs):
    refs = list(refs)

    def take(n):
        out = refs[:n]
        del refs[:n]
        return out

    hidden_in = take(3)
    (peaks,) = take(1)
    down_land = take(3)
    (out,) = take(1)
    hidden, down_w, sent, landed = (take(3) for _ in range(4))
    acc, total, send_sems, recv_sems, own_sems = take(5)
    toks, feat = out.shape
    quarter, slab = toks // 4, toks // 16
    xyz, core = place()
    other = 1 - core

    partners = [device_at(xyz, other)]
    for axis in range(3):
        for step in range(1, SIDE):
            partners.append(device_at(moved(xyz, axis, step), core))
    greet(partners)

    mail = Mail(send_sems, recv_sems)
    slab_in, own = [[], [], []], []
    for g in range(3):
        b_axis, c_axis = SUM_AXES[g]
        row = mult(xyz[b_axis] * quarter + xyz[c_axis] * slab, slab)
        home = hidden[g].at[core, pl.ds(row, slab), :]
        for step in (2, 1, 3):
            slab_in[g].append(
                mail.post(hidden_in[g], home, device_at(moved(xyz, c_axis, step), core))
            )
        copy = pltpu.make_async_copy(hidden_in[g], home, own_sems.at[g])
        copy.start()
        own.append(copy)
    for g in range(3):
        copy = pltpu.make_async_copy(down_land[g], down_w[g], own_sems.at[3 + g])
        copy.start()
        own.append(copy)
    factor = jnp.max(127.0 / peaks[2:3, :])
    unit = jnp.max(peaks[2:3, :] / 127.0)

    quarter_in, cross_in = [[], [], []], [[], [], []]

    def cross(g, step):
        b_axis = SUM_AXES[g][0]
        from_b = lax.rem(xyz[b_axis] + SIDE - step, SIDE)
        view = hidden[g].at[core, pl.ds(mult(from_b * quarter, quarter), quarter), :]
        cross_in[g].append(mail.post(view, view, device_at(xyz, other)))

    for g in range(3):
        b_axis = SUM_AXES[g][0]
        for copy in slab_in[g]:
            copy.wait_recv()
        own[g].wait()
        view = hidden[g].at[core, pl.ds(mult(xyz[b_axis] * quarter, quarter), quarter), :]
        for step in (2, 1, 3):
            quarter_in[g].append(
                mail.post(view, view, device_at(moved(xyz, b_axis, step), core))
            )
        cross(g, 0)
    for g in range(3):
        own[3 + g].wait()
        scale_rows(down_w[g], 2 * widths[g], 4 * feat, factor)
    landed_in = [[], [], []]
    for g in range(3):
        for copy, step in zip(quarter_in[g], (2, 1, 3)):
            copy.wait_recv()
            cross(g, step)
    for g in range(3):
        for copy in cross_in[g]:
            copy.wait_recv()
        width = widths[g]

        def body(i, carry, g=g, width=width):
            rows = pl.ds(mult(i * quarter, quarter), quarter)
            value = jnp.dot(
                hidden[g][0, rows, :], down_w[g][pl.ds(0, width), :],
                preferred_element_type=jnp.float32,
            ) + jnp.dot(
                hidden[g][1, rows, :], down_w[g][pl.ds(width, width), :],
                preferred_element_type=jnp.float32,
            )
            for j in range(SIDE):
                block = value[:, j * feat : (j + 1) * feat]
                acc[j, rows, :] = block
                sent[g][j, rows, :] = block.astype(jnp.bfloat16)
            mine = acc[xyz[g], rows, :]
            if g == 0:
                total[rows, :] = mine
            else:
                total[rows, :] = total[rows, :] + mine
            return carry

        lax.fori_loop(0, SIDE, body, 0)
        for step in (2, 1, 3):
            there = moved(xyz, g, step)
            landed_in[g].append(
                mail.post(sent[g].at[there[g]], landed[g].at[step - 1], device_at(there, core))
            )
    for g in range(3):
        for copy in landed_in[g]:
            copy.wait_recv()
    value = total[...]
    for g in range(3):
        for n in range(3):
            value = value + landed[g][n].astype(jnp.float32)
    out[...] = (value * unit).astype(jnp.bfloat16)
    mail.finish()


def shards(tokens, gate_weight, up_weight, down_weight):
    toks, feat = tokens.shape
    ff = gate_weight.shape[1]
    widths = class_widths(ff)
    bases = class_bases(widths)
    quarter, slab = toks // 4, toks // 16
    bf16, f32 = jnp.bfloat16, jnp.float32
    hbm = pl.BlockSpec(memory_space=pl.ANY)
    vmem = pl.BlockSpec(memory_space=pltpu.VMEM)
    shape = jax.ShapeDtypeStruct

    scratch = [pltpu.VMEM((8 * feat, w), bf16) for w in widths] * 2
    scratch += [pltpu.VMEM((toks, 8 * feat), bf16) for _ in widths]
    scratch += [pltpu.VMEM((2, toks, w), bf16) for w in widths]
    scratch += [pltpu.VMEM((2, 3, quarter, w), bf16) for w in widths]
    scratch += [pltpu.VMEM((2, quarter, w), f32) for w in widths]
    scratch += [pltpu.VMEM((2, 3, slab, w), f32) for w in widths]
    scratch += [
        pltpu.VMEM((toks, 384), f32),
        pltpu.VMEM((3, 8, 128), f32),
        pltpu.VMEM((13, 8, 128), f32),
        pltpu.SemaphoreType.DMA((121,)),
        pltpu.SemaphoreType.DMA((121,)),
        pltpu.SemaphoreType.DMA((12,)),
        pltpu.SemaphoreType.DMA((36,)),
    ]
    outs = pl.pallas_call(
        functools.partial(kernel_in, widths, bases),
        out_shape=(
            *[shape((slab, w), bf16) for w in widths],
            shape((8, 128), f32),
            *[shape((2 * w, 4 * feat), bf16) for w in widths],
        ),
        in_specs=[hbm] * 4,
        out_specs=(vmem, vmem, vmem, vmem, hbm, hbm, hbm),
        scratch_shapes=scratch,
        compiler_params=pltpu.CompilerParams(
            collective_id=0, has_side_effects=True, vmem_limit_bytes=60 * 2**20
        ),
        name="refit_in",
    )(tokens, gate_weight, up_weight, down_weight)
    hidden, peaks, down_land = outs[:3], outs[3], outs[4:]

    scratch = [pltpu.VMEM((2, toks, w), bf16) for w in widths]
    scratch += [pltpu.VMEM((2 * w, 4 * feat), bf16) for w in widths]
    scratch += [pltpu.VMEM((SIDE, toks, feat), bf16) for w in widths]
    scratch += [pltpu.VMEM((3, toks, feat), bf16) for w in widths]
    scratch += [
        pltpu.VMEM((SIDE, toks, feat), f32),
        pltpu.VMEM((toks, feat), f32),
        pltpu.SemaphoreType.DMA((39,)),
        pltpu.SemaphoreType.DMA((39,)),
        pltpu.SemaphoreType.DMA((6,)),
    ]
    output_block = pl.pallas_call(
        functools.partial(kernel_out, widths),
        out_shape=shape((toks, feat), bf16),
        in_specs=[vmem] * 4 + [hbm] * 3,
        out_specs=vmem,
        scratch_shapes=scratch,
        compiler_params=pltpu.CompilerParams(
            collective_id=1, has_side_effects=True, vmem_limit_bytes=60 * 2**20
        ),
        name="refit_out",
    )(*hidden, peaks, *down_land)
    return output_block, peaks[:3, 0]


def solution(mesh):
    in_specs = (
        P(None, ("rep", "tp")),
        P(("rep", "tp"), None),
        P(("rep", "tp"), None),
        P(None, ("rep", "tp")),
    )
    out_specs = (P(None, ("rep", "tp")), P())
    return jax.shard_map(shards, mesh=mesh, in_specs=in_specs, out_specs=out_specs, check_vma=False)
```

```python
import functools

import jax
import jax.numpy as jnp
from jax import lax
from jax.experimental import pallas as pl
from jax.experimental.pallas import tpu as pltpu
from jax.sharding import PartitionSpec as P

MESH = pl.DeviceIdType.MESH
SIDE = 4
SUM_AXES = ((1, 2), (2, 0), (0, 1))


def class_widths(ff):
    units = ff // (8 * 128)
    first = (units + 2) // 3
    second = (units - first + 1) // 2
    return [first * 128, second * 128, (units - first - second) * 128]


def class_bases(widths):
    return [0, 8 * widths[0], 8 * (widths[0] + widths[1])]


def place():
    rep = lax.axis_index("rep")
    tp = lax.axis_index("tp")
    return (rep // SIDE, tp // 2, lax.rem(rep, SIDE)), lax.rem(tp, 2)


def device_at(xyz, core):
    return (xyz[0] * SIDE + xyz[2], xyz[1] * 2 + core)


def moved(xyz, axis, step):
    out = list(xyz)
    out[axis] = lax.rem(xyz[axis] + step, SIDE)
    return tuple(out)


def mult(value, of):
    return pl.multiple_of(value, of)


class Mail:
    def __init__(self, send_sems, recv_sems):
        self.send_sems, self.recv_sems, self.used, self.sent = send_sems, recv_sems, 0, []

    def post(self, src, dst, device):
        copy = pltpu.make_async_remote_copy(
            src_ref=src,
            dst_ref=dst,
            send_sem=self.send_sems.at[self.used],
            recv_sem=self.recv_sems.at[self.used],
            device_id=device,
            device_id_type=MESH,
        )
        self.used += 1
        copy.start()
        self.sent.append(copy)
        return copy

    def finish(self):
        for copy in self.sent:
            copy.wait_send()


def greet(partners):
    barrier = pltpu.get_barrier_semaphore()
    for partner in partners:
        pl.semaphore_signal(barrier, inc=1, device_id=partner, device_id_type=MESH)
    pl.semaphore_wait(barrier, len(partners))


def scale_rows(ref, rows, columns, factor, step=32):
    def body(i, carry):
        at = pl.ds(mult(i * step, step), step)
        wide = ref[at, :].astype(jnp.float32)
        ref[at, :] = jnp.floor(wide * factor + 0.5).astype(jnp.bfloat16)
        return carry

    lax.fori_loop(0, rows // step, body, 0)


def kernel(widths, bases, tokens, gate, up, down, *refs):
    refs = list(refs)

    def take(n):
        out = refs[:n]
        del refs[:n]
        return out

    out, peaks_out = take(2)
    down_land = take(3)
    gate_w, up_w, tok, part, near, half, total, far, hidden, sent, landed = (
        take(3) for _ in range(11)
    )
    acc, blocks, mine_out, peak_send, peak_recv = take(5)
    send_sems, recv_sems, own_sems, load_sems = take(4)
    toks, feat = tokens.shape
    quarter, slab = toks // 4, toks // 16
    mid = quarter // 2
    xyz, core = place()
    other = 1 - core
    mail = Mail(send_sems, recv_sems)

    def load(source, spots, first):
        copies = []
        for g in range(3):
            if source is down:
                pieces = 2 * (widths[g] // feat)
            else:
                pieces = 8
            for p in range(pieces):
                if source is down:
                    rows = 4 * feat
                    start = bases[g] + p * rows
                    view = spots[g].at[
                        p % 2, pl.ds(0, rows), pl.ds((p // 2) * feat, feat)
                    ]
                    origin = source.at[pl.ds(start, rows), :]
                else:
                    view = spots[g].at[p // 4, pl.ds((p % 4) * feat, feat), :]
                    origin = source.at[:, pl.ds(bases[g] + p * widths[g], widths[g])]
                copies.append(
                    pltpu.make_async_copy(origin, view, load_sems.at[first + len(copies)])
                )
        for copy in copies:
            copy.start()
        return copies

    def top_of(spots, copies):
        for copy in copies:
            copy.wait()
        best = None
        for g in range(3):

            def body(i, carry, g=g):
                at = pl.ds(mult(i * 32, 32), 32)
                return jnp.maximum(
                    carry, jnp.maximum(jnp.abs(spots[g][0, at, :]), jnp.abs(spots[g][1, at, :]))
                )

            high = lax.fori_loop(
                0, 4 * feat // 32, body, jnp.zeros((32, widths[g]), jnp.bfloat16)
            )
            high = jnp.max(high.astype(jnp.float32))
            best = high if best is None else jnp.maximum(best, high)
        return best

    gate_load = load(gate, part, 0)
    up_load = load(up, hidden, 24)

    own = {}

    def keep(name, src, dst, sem):
        copy = pltpu.make_async_copy(src, dst, own_sems.at[sem])
        copy.start()
        own[name] = copy

    def token_spot(g, position, c):
        return tok[g].at[:, pl.ds(mult((position * 2 + c) * feat, feat), feat)]

    def weight_spot(kind, g):
        slot = mult((xyz[g] * 2 + core) * feat, feat)
        return (gate_w, up_w)[kind][g].at[pl.ds(slot, feat), pl.ds(0, widths[g])]

    def weight_part(kind, g, position, c):
        col = mult(bases[g] + (position * 2 + c) * widths[g], 128)
        return (gate, up)[kind].at[:, pl.ds(col, widths[g])]

    for g in range(3):
        keep(("tok", g), tokens, token_spot(g, xyz[g], core), g)
        for kind in range(2):
            keep((kind, g), weight_part(kind, g, xyz[g], core), weight_spot(kind, g), 3 + 2 * g + kind)

    partners = [device_at(xyz, other)]
    for axis in range(3):
        for step in range(1, SIDE):
            for c in range(2):
                partners.append(device_at(moved(xyz, axis, step), c))
    greet(partners)

    tok_in, tok_cross = [[], [], []], [[], [], []]
    for step in (2, 1, 3):
        for g in range(3):
            tok_in[g].append(
                (
                    step,
                    mail.post(
                        tokens, token_spot(g, xyz[g], core), device_at(moved(xyz, g, step), core)
                    ),
                )
            )
    for g in range(3):
        tok_cross[g].append(
            mail.post(tokens, token_spot(g, xyz[g], core), device_at(xyz, other))
        )

    weight_in = {}

    def send_weights(kind, step, flip):
        for g in range(3):
            there = moved(xyz, g, step)
            c = core if flip == 0 else other
            weight_in.setdefault((kind, g), []).append(
                mail.post(
                    weight_part(kind, g, there[g], c), weight_spot(kind, g), device_at(there, c)
                )
            )

    gate_top = top_of(part, gate_load)
    down_load = load(down, part, 48)
    up_top = top_of(hidden, up_load)
    down_top = top_of(part, down_load)
    row = lax.broadcasted_iota(jnp.int32, (8, 128), 0)
    tile = jnp.where(row == 0, gate_top, jnp.where(row == 1, up_top, down_top))

    got = 0
    for axis in range(3):
        peak_send[axis] = tile
        waits = []
        for step in range(SIDE):
            for flip in range(2):
                if step == 0 and flip == 0 or axis > 0 and flip == 1:
                    continue
                there = device_at(moved(xyz, axis, step), core if flip == 0 else other)
                waits.append((got, mail.post(peak_send.at[axis], peak_recv.at[got], there)))
                got += 1
        if axis < 2:
            send_weights(0, 1, axis)
            send_weights(0, 3, axis)
        else:
            send_weights(0, 2, 0)
            send_weights(0, 2, 1)
            send_weights(0, 0, 1)
            for flip in range(2):
                for step in (2, 1, 3):
                    send_weights(1, step, flip)
            send_weights(1, 0, 1)
        if axis == 1:
            for g in range(3):
                for step, copy in tok_in[g]:
                    copy.wait_recv()
                    spot = token_spot(g, lax.rem(xyz[g] + SIDE - step, SIDE), core)
                    tok_cross[g].append(mail.post(spot, spot, device_at(xyz, other)))
        for n, copy in waits:
            copy.wait_recv()
            tile = jnp.maximum(tile, peak_recv[n])
    peaks_out[...] = tile
    factors = [jnp.max(127.0 / tile[k : k + 1, :]) for k in range(3)]
    units = [jnp.max(tile[k : k + 1, :] / 127.0) for k in range(3)]

    def partial_sums(kind, g):
        width = widths[g]
        cols = 384 if width % 384 == 0 else 256 if width % 256 == 0 else 128
        b = xyz[SUM_AXES[g][0]]
        weights = (gate_w, up_w)[kind][g]

        def body(j, carry):
            at = pl.ds(mult(j * cols, 128), cols)
            acc[:, pl.ds(0, cols)] = jnp.dot(
                tok[g][...], weights[pl.ds(0, 8 * feat), at], preferred_element_type=jnp.float32
            )
            part[g][kind, :, at] = acc[:, pl.ds(0, cols)].astype(jnp.bfloat16)
            mine = pl.ds(mult(b * quarter, quarter), quarter)
            total[g][kind, :, at] = acc[mine, pl.ds(0, cols)]
            return carry

        lax.fori_loop(0, width // cols, body, 0)

    near_in, half_in = {}, {}

    def rows_of(position, first, count):
        return pl.ds(mult(position * quarter + first, 16), count)

    def send_near(kind, g):
        axis = SUM_AXES[g][0]
        after, before, far_off = (moved(xyz, axis, s) for s in (1, 3, 2))
        half_in[kind, g] = [
            mail.post(
                part[g].at[kind, rows_of(far_off[axis], 0, mid), :],
                half[g].at[kind, 0],
                device_at(after, core),
            ),
            mail.post(
                part[g].at[kind, rows_of(far_off[axis], mid, mid), :],
                half[g].at[kind, 1],
                device_at(before, core),
            ),
        ]
        near_in[kind, g] = [
            mail.post(
                part[g].at[kind, rows_of(after[axis], mid, mid), :],
                near[g].at[kind, 0, pl.ds(mid, mid), :],
                device_at(after, core),
            ),
            mail.post(
                part[g].at[kind, rows_of(before[axis], 0, mid), :],
                near[g].at[kind, 1, pl.ds(0, mid), :],
                device_at(before, core),
            ),
        ]

    def pass_near(kind, g):
        axis = SUM_AXES[g][0]
        for n, (step, first) in enumerate(((1, 0), (3, mid))):
            there = moved(xyz, axis, step)
            half_in[kind, g][n].wait_recv()

            def body(i, carry, n=n, first=first, there=there):
                at = rows_of(there[axis], first + i * 16, 16)
                value = part[g][kind, at, :].astype(jnp.float32) + half[g][
                    kind, n, pl.ds(mult(i * 16, 16), 16), :
                ].astype(jnp.float32)
                part[g][kind, at, :] = value.astype(jnp.bfloat16)
                return carry

            lax.fori_loop(0, mid // 16, body, 0)
            near_in[kind, g].append(
                mail.post(
                    part[g].at[kind, rows_of(there[axis], first, mid), :],
                    near[g].at[kind, n, pl.ds(first, mid), :],
                    device_at(there, core),
                )
            )

    down_in = [[], [], []]

    def send_down(step):
        for g in range(3):
            there = moved(xyz, g, step)
            start = mult(bases[g] + there[g] * 2 * widths[g], 128)
            src = down.at[pl.ds(start, 2 * widths[g]), :]
            dst = down_land[g].at[:, pl.ds(mult(xyz[g] * feat, feat), feat)]
            if step == 0:
                keep(("down", g), src, dst, 9 + g)
            else:
                down_in[g].append(mail.post(src, dst, device_at(there, core)))

    for kind in range(2):
        for g in range(3):
            for copy in weight_in[kind, g]:
                copy.wait_recv()
            own[kind, g].wait()
            scale_rows((gate_w, up_w)[kind][g], 8 * feat, widths[g], factors[kind])
            if kind == 0:
                for copy in tok_cross[g]:
                    copy.wait_recv()
                own["tok", g].wait()
            partial_sums(kind, g)
            send_near(kind, g)
    send_down(0)
    for kind in range(2):
        for g in range(3):
            pass_near(kind, g)
    send_down(1)
    send_down(3)

    far_in = [[], [], []]
    for kind in range(2):
        for g in range(3):
            axis = SUM_AXES[g][1]
            for copy in near_in[kind, g]:
                copy.wait_recv()

            def body(i, carry, kind=kind, g=g):
                at = pl.ds(mult(i * 16, 16), 16)
                total[g][kind, at, :] = total[g][kind, at, :] + (
                    near[g][kind, 0, at, :].astype(jnp.float32)
                    + near[g][kind, 1, at, :].astype(jnp.float32)
                )
                return carry

            lax.fori_loop(0, quarter // 16, body, 0)
            for step in (2, 1, 3):
                there = moved(xyz, axis, step)
                rows = pl.ds(mult(there[axis] * slab, slab), slab)
                far_in[g].append(
                    mail.post(
                        total[g].at[kind, rows, :],
                        far[g].at[kind, step - 1],
                        device_at(there, core),
                    )
                )
    send_down(2)

    slab_in = [[], [], []]
    for g in range(3):
        b_axis, c_axis = SUM_AXES[g]
        for copy in far_in[g]:
            copy.wait_recv()
        start = xyz[b_axis] * quarter + xyz[c_axis] * slab

        def body(i, carry, g=g, c_axis=c_axis, start=start):
            at = pl.ds(mult(i * 16, 16), 16)
            mine = pl.ds(mult(xyz[c_axis] * slab + i * 16, 16), 16)
            sums = []
            for kind in range(2):
                value = (total[g][kind, mine, :] + far[g][kind, 1, at, :]) + (
                    far[g][kind, 0, at, :] + far[g][kind, 2, at, :]
                )
                sums.append(value * units[kind])
            value = sums[0] / (1.0 + jnp.exp(-sums[0])) * sums[1]
            hidden[g][core, pl.ds(mult(start + i * 16, 16), 16), :] = value.astype(jnp.bfloat16)
            return carry

        lax.fori_loop(0, slab // 16, body, 0)
        home = hidden[g].at[core, pl.ds(mult(start, slab), slab), :]
        for step in (2, 1, 3):
            slab_in[g].append(mail.post(home, home, device_at(moved(xyz, c_axis, step), core)))

    quarter_in, rest_in, cross_in = [[], [], []], [[], [], []], [[], [], []]

    def hidden_rows(g, step, first, count):
        position = lax.rem(xyz[SUM_AXES[g][0]] + step, SIDE)
        return hidden[g].at[core, rows_of(position, first, count), :]

    def cross(g, step):
        view = hidden_rows(g, step, 0, quarter)
        cross_in[g].append(mail.post(view, view, device_at(xyz, other)))

    for g in range(3):
        axis = SUM_AXES[g][0]
        for copy in slab_in[g]:
            copy.wait_recv()
        view = hidden_rows(g, 0, 0, quarter)
        for step in (1, 3):
            quarter_in[g].append(mail.post(view, view, device_at(moved(xyz, axis, step), core)))
        cross(g, 0)

    for g in range(3):
        for copy in down_in[g]:
            copy.wait_recv()
        own["down", g].wait()
        for p in range(2):
            keep(
                ("down", g, p),
                down_land[g].at[pl.ds(p * widths[g], widths[g]), :],
                gate_w[g].at[pl.ds(0, widths[g]), pl.ds(p * 4 * feat, 4 * feat)],
                12 + 2 * g + p,
            )
    mine_out[...] = jnp.zeros_like(mine_out)
    for g in range(3):
        for p in range(2):
            own["down", g, p].wait()
        scale_rows(gate_w[g], widths[g], 8 * feat, factors[2])

    for g in range(3):
        axis = SUM_AXES[g][0]
        quarter_in[g][0].wait_recv()
        view = hidden_rows(g, 3, 0, mid)
        rest_in[g].append(mail.post(view, view, device_at(moved(xyz, axis, 1), core)))
        quarter_in[g][1].wait_recv()
        view = hidden_rows(g, 1, mid, mid)
        rest_in[g].append(mail.post(view, view, device_at(moved(xyz, axis, 3), core)))
        cross(g, 3)
        cross(g, 1)

    landed_in = []

    def output_rows(g, n, step):
        cross_in[g][n].wait_recv()
        width = widths[g]
        rows = rows_of(lax.rem(xyz[SUM_AXES[g][0]] + step, SIDE), 0, quarter)
        value = jnp.dot(
            hidden[g][0, rows, :], gate_w[g][pl.ds(0, width), pl.ds(0, 4 * feat)],
            preferred_element_type=jnp.float32,
        ) + jnp.dot(
            hidden[g][1, rows, :], gate_w[g][pl.ds(0, width), pl.ds(4 * feat, 4 * feat)],
            preferred_element_type=jnp.float32,
        )
        for j in range(SIDE):
            block = value[:, j * feat : (j + 1) * feat]
            blocks[j] = block
            sent[g][j, rows, :] = block.astype(jnp.bfloat16)
        mine_out[rows, :] = mine_out[rows, :] + blocks[xyz[g]]
        for step in (2, 1, 3):
            there = moved(xyz, g, step)
            landed_in.append(
                mail.post(
                    sent[g].at[there[g], rows, :],
                    landed[g].at[step - 1, rows, :],
                    device_at(there, core),
                )
            )

    for n, step in ((0, 0), (1, 3), (2, 1)):
        for g in range(3):
            output_rows(g, n, step)
    for g in range(3):
        for copy in rest_in[g]:
            copy.wait_recv()
        cross(g, 2)
    for g in range(3):
        output_rows(g, 3, 2)
    for copy in landed_in:
        copy.wait_recv()
    value = mine_out[...]
    for g in range(3):
        for n in range(3):
            value = value + landed[g][n].astype(jnp.float32)
    out[...] = (value * units[2]).astype(jnp.bfloat16)
    mail.finish()


def shards(tokens, gate_weight, up_weight, down_weight):
    toks, feat = tokens.shape
    ff = gate_weight.shape[1]
    widths = class_widths(ff)
    bases = class_bases(widths)
    quarter, slab = toks // 4, toks // 16
    bf16, f32 = jnp.bfloat16, jnp.float32
    hbm = pl.BlockSpec(memory_space=pl.ANY)
    vmem = pl.BlockSpec(memory_space=pltpu.VMEM)
    shape = jax.ShapeDtypeStruct

    scratch = [pltpu.VMEM((max(8 * feat, w), max(8 * feat, w)), bf16) for w in widths]
    scratch += [pltpu.VMEM((8 * feat, w), bf16) for w in widths]
    scratch += [pltpu.VMEM((toks, 8 * feat), bf16) for _ in widths]
    scratch += [pltpu.VMEM((2, toks, w), bf16) for w in widths]
    scratch += [pltpu.VMEM((2, 2, quarter, w), bf16) for w in widths]
    scratch += [pltpu.VMEM((2, 2, quarter // 2, w), bf16) for w in widths]
    scratch += [pltpu.VMEM((2, quarter, w), f32) for w in widths]
    scratch += [pltpu.VMEM((2, 3, slab, w), f32) for w in widths]
    scratch += [pltpu.VMEM((2, toks, w), bf16) for w in widths]
    scratch += [pltpu.VMEM((SIDE, toks, feat), bf16) for _ in widths]
    scratch += [pltpu.VMEM((3, toks, feat), bf16) for _ in widths]
    scratch += [
        pltpu.VMEM((toks, 384), f32),
        pltpu.VMEM((SIDE, quarter, feat), f32),
        pltpu.VMEM((toks, feat), f32),
        pltpu.VMEM((3, 8, 128), f32),
        pltpu.VMEM((13, 8, 128), f32),
        pltpu.SemaphoreType.DMA((208,)),
        pltpu.SemaphoreType.DMA((208,)),
        pltpu.SemaphoreType.DMA((18,)),
        pltpu.SemaphoreType.DMA((100,)),
    ]
    outs = pl.pallas_call(
        functools.partial(kernel, widths, bases),
        out_shape=(
            shape((toks, feat), bf16),
            shape((8, 128), f32),
            *[shape((2 * w, 4 * feat), bf16) for w in widths],
        ),
        in_specs=[hbm] * 4,
        out_specs=(vmem, vmem, hbm, hbm, hbm),
        scratch_shapes=scratch,
        compiler_params=pltpu.CompilerParams(
            collective_id=0, has_side_effects=True, vmem_limit_bytes=63 * 2**20
        ),
        name="refit",
    )(tokens, gate_weight, up_weight, down_weight)
    return outs[0], outs[1][:3, 0]


def solution(mesh):
    in_specs = (
        P(None, ("rep", "tp")),
        P(("rep", "tp"), None),
        P(("rep", "tp"), None),
        P(None, ("rep", "tp")),
    )
    out_specs = (P(None, ("rep", "tp")), P())
    return jax.shard_map(shards, mesh=mesh, in_specs=in_specs, out_specs=out_specs, check_vma=False)
```

```python
import functools

import jax
import jax.numpy as jnp
from jax import lax
from jax.experimental import pallas as pl
from jax.experimental.pallas import tpu as pltpu
from jax.sharding import PartitionSpec as P

MESH = pl.DeviceIdType.MESH
SIDE = 4
SUM_AXES = ((1, 2), (2, 0), (0, 1))


def class_widths(ff):
    units = ff // (8 * 128)
    first = (units + 2) // 3
    second = (units - first + 1) // 2
    return [first * 128, second * 128, (units - first - second) * 128]


def class_bases(widths):
    return [0, 8 * widths[0], 8 * (widths[0] + widths[1])]


def place():
    rep = lax.axis_index("rep")
    tp = lax.axis_index("tp")
    return (rep // SIDE, tp // 2, lax.rem(rep, SIDE)), lax.rem(tp, 2)


def device_at(xyz, core):
    return (xyz[0] * SIDE + xyz[2], xyz[1] * 2 + core)


def moved(xyz, axis, step):
    out = list(xyz)
    out[axis] = lax.rem(xyz[axis] + step, SIDE)
    return tuple(out)


def mult(value, of):
    return pl.multiple_of(value, of)


class Mail:
    def __init__(self, send_sems, recv_sems):
        self.send_sems, self.recv_sems, self.used, self.sent = send_sems, recv_sems, 0, []

    def post(self, src, dst, device):
        copy = pltpu.make_async_remote_copy(
            src_ref=src,
            dst_ref=dst,
            send_sem=self.send_sems.at[self.used],
            recv_sem=self.recv_sems.at[self.used],
            device_id=device,
            device_id_type=MESH,
        )
        self.used += 1
        copy.start()
        self.sent.append(copy)
        return copy

    def settle(self, copies):
        for copy in copies:
            copy.wait_send()
        self.sent = [copy for copy in self.sent if not any(copy is c for c in copies)]

    def finish(self):
        for copy in self.sent:
            copy.wait_send()


def greet(partners):
    for partner in partners:
        pl.semaphore_signal(
            pltpu.get_barrier_semaphore(), inc=1, device_id=partner, device_id_type=MESH
        )


def scale_rows(ref, rows, factor, step=32):
    def body(i, carry):
        at = pl.ds(mult(i * step, step), step)
        wide = ref[at, :].astype(jnp.float32)
        ref[at, :] = jnp.floor(wide * factor + 0.5).astype(jnp.bfloat16)
        return carry

    lax.fori_loop(0, rows // step, body, 0)


def scale_block(ref, rows, col, cols, factor, step=64):
    def body(i, carry):
        at = pl.ds(mult(i * step, step), step)
        wide = ref[at, pl.ds(col, cols)].astype(jnp.float32)
        ref[at, pl.ds(col, cols)] = jnp.floor(wide * factor + 0.5).astype(jnp.bfloat16)
        return carry

    lax.fori_loop(0, rows // step, body, 0)


def kernel(widths, bases, tokens, gate, up, down, *refs):
    refs = list(refs)

    def take(n):
        out = refs[:n]
        del refs[:n]
        return out

    out, peaks_out = take(2)
    down_land = take(3)
    gate_w, up_w, tok, part, near, half, total, far, far_half, hidden, sent, landed = (
        take(3) for _ in range(12)
    )
    acc, blocks, mine_out, peak_send, peak_recv = take(5)
    send_sems, recv_sems, own_sems, load_sems = take(4)
    toks, feat = tokens.shape
    quarter, slab = toks // 4, toks // 16
    mid = quarter // 2
    xyz, core = place()
    other = 1 - core
    mail = Mail(send_sems, recv_sems)

    partners = [device_at(xyz, other)]
    for axis in range(3):
        for step in range(1, SIDE):
            for c in range(2):
                partners.append(device_at(moved(xyz, axis, step), c))
    greet(partners)

    def load(source, spots, first):
        copies = []
        for g in range(3):
            if source is down:
                pieces = 2 * (widths[g] // feat)
            else:
                pieces = 8
            for p in range(pieces):
                if source is down:
                    rows = 4 * feat
                    start = bases[g] + p * rows
                    view = spots[g].at[
                        p % 2, pl.ds(0, rows), pl.ds((p // 2) * feat, feat)
                    ]
                    origin = source.at[pl.ds(start, rows), :]
                else:
                    view = spots[g].at[p // 4, pl.ds((p % 4) * feat, feat), :]
                    origin = source.at[:, pl.ds(bases[g] + p * widths[g], widths[g])]
                copies.append(
                    pltpu.make_async_copy(origin, view, load_sems.at[first + len(copies)])
                )
        for copy in copies:
            copy.start()
        return copies

    def top_of(spots, copies):
        for copy in copies:
            copy.wait()
        best = None
        for g in range(3):

            def body(i, carry, g=g):
                at = pl.ds(mult(i * 32, 32), 32)
                return jnp.maximum(
                    carry, jnp.maximum(jnp.abs(spots[g][0, at, :]), jnp.abs(spots[g][1, at, :]))
                )

            high = lax.fori_loop(
                0, 4 * feat // 32, body, jnp.zeros((32, widths[g]), jnp.bfloat16)
            )
            high = jnp.max(high.astype(jnp.float32))
            best = high if best is None else jnp.maximum(best, high)
        return best

    gate_load = load(gate, part, 0)

    own = {}

    def keep(name, src, dst, sem):
        copy = pltpu.make_async_copy(src, dst, own_sems.at[sem])
        copy.start()
        own[name] = copy

    def token_spot(g, position, c):
        return tok[g].at[:, pl.ds(mult((position * 2 + c) * feat, feat), feat)]

    def weight_spot(kind, g):
        slot = mult((xyz[g] * 2 + core) * feat, feat)
        return (gate_w, up_w)[kind][g].at[pl.ds(slot, feat), pl.ds(0, widths[g])]

    def weight_part(kind, g, position, c):
        col = mult(bases[g] + (position * 2 + c) * widths[g], 128)
        return (gate, up)[kind].at[:, pl.ds(col, widths[g])]

    pl.semaphore_wait(pltpu.get_barrier_semaphore(), len(partners))

    tok_in, tok_rest, tok_cross = ([[], [], []] for _ in range(3))

    def cross_tokens(g, step):
        spot = token_spot(g, lax.rem(xyz[g] + step, SIDE), core)
        tok_cross[g].append(mail.post(spot, spot, device_at(xyz, other)))

    for step in (1, 3):
        for g in range(3):
            there = device_at(moved(xyz, g, step), core)
            tok_in[g].append(mail.post(tokens, token_spot(g, xyz[g], core), there))
    for g in range(3):
        tok_cross[g].append(
            mail.post(tokens, token_spot(g, xyz[g], core), device_at(xyz, other))
        )

    def pass_tokens(g):
        for n, (back, on) in enumerate(((3, 1), (1, 3))):
            tok_in[g][n].wait_recv()
            slot = mult((lax.rem(xyz[g] + back, SIDE) * 2 + core) * feat, feat)
            view = tok[g].at[pl.ds(n * (toks // 2), toks // 2), pl.ds(slot, feat)]
            tok_rest[g].append(mail.post(view, view, device_at(moved(xyz, g, on), core)))
        cross_tokens(g, 3)
        cross_tokens(g, 1)

    weight_in = {}

    def send_weights(kind, step, flip):
        for g in range(3):
            there = moved(xyz, g, step)
            c = core if flip == 0 else other
            weight_in.setdefault((kind, g), []).append(
                mail.post(
                    weight_part(kind, g, there[g], c), weight_spot(kind, g), device_at(there, c)
                )
            )

    send_weights(0, 1, 0)
    send_weights(0, 3, 0)
    up_load = load(up, hidden, 24)
    for g in range(3):
        keep(("tok", g), tokens, token_spot(g, xyz[g], core), g)
        for kind in range(2):
            keep((kind, g), weight_part(kind, g, xyz[g], core), weight_spot(kind, g), 3 + 2 * g + kind)
    gate_top = top_of(part, gate_load)
    down_load = load(down, part, 48)
    up_top = top_of(hidden, up_load)
    down_top = top_of(part, down_load)
    row = lax.broadcasted_iota(jnp.int32, (8, 128), 0)
    tile = jnp.where(row == 0, gate_top, jnp.where(row == 1, up_top, down_top))

    got = 0
    for axis in range(3):
        peak_send[axis] = tile
        waits = []
        for step in range(SIDE):
            for flip in range(2):
                if step == 0 and flip == 0 or axis > 0 and flip == 1:
                    continue
                there = device_at(moved(xyz, axis, step), core if flip == 0 else other)
                waits.append((got, mail.post(peak_send.at[axis], peak_recv.at[got], there)))
                got += 1
        if axis == 0:
            send_weights(0, 1, 1)
            send_weights(0, 3, 1)
        elif axis == 1:
            for g in range(3):
                pass_tokens(g)
            send_weights(0, 2, 0)
        else:
            send_weights(0, 2, 1)
            send_weights(0, 0, 1)
            for flip in range(2):
                for step in (2, 1, 3):
                    send_weights(1, step, flip)
            send_weights(1, 0, 1)
            for g in range(3):
                for copy in tok_rest[g]:
                    copy.wait_recv()
                cross_tokens(g, 2)
        for n, copy in waits:
            copy.wait_recv()
            tile = jnp.maximum(tile, peak_recv[n])
    peaks_out[...] = tile
    factors = [jnp.max(127.0 / tile[k : k + 1, :]) for k in range(3)]
    units = [jnp.max(tile[k : k + 1, :] / 127.0) for k in range(3)]

    def partial_sums(kind, g):
        width = widths[g]
        cols = 384 if width % 384 == 0 else 256 if width % 256 == 0 else 128
        b = xyz[SUM_AXES[g][0]]
        weights = (gate_w, up_w)[kind][g]

        def body(j, carry):
            at = pl.ds(mult(j * cols, 128), cols)
            acc[:, pl.ds(0, cols)] = jnp.dot(
                tok[g][...], weights[pl.ds(0, 8 * feat), at], preferred_element_type=jnp.float32
            )
            part[g][kind, :, at] = acc[:, pl.ds(0, cols)].astype(jnp.bfloat16)
            mine = pl.ds(mult(b * quarter, quarter), quarter)
            total[g][kind, :, at] = acc[mine, pl.ds(0, cols)]
            return carry

        lax.fori_loop(0, width // cols, body, 0)

    def ring_rows(position, size, first, count):
        return pl.ds(mult(position * size + first, 8 if size == slab else 16), count)

    def send_ring(src, whole, piece, axis, kind, size):
        cut = size // 2
        after, before, far_off = (moved(xyz, axis, s) for s in (1, 3, 2))
        pieces = [
            mail.post(
                src.at[kind, ring_rows(far_off[axis], size, n * cut, cut), :],
                piece.at[kind, n],
                device_at(there, core),
            )
            for n, there in enumerate((after, before))
        ]
        wholes = [
            mail.post(
                src.at[kind, ring_rows(there[axis], size, (1 - n) * cut, cut), :],
                whole.at[kind, n, pl.ds((1 - n) * cut, cut), :],
                device_at(there, core),
            )
            for n, there in enumerate((after, before))
        ]
        return pieces, wholes

    def pass_ring(src, whole, piece, axis, kind, size, posts):
        cut = size // 2
        pieces, wholes = posts
        step = 16 if cut % 16 == 0 else 8
        for n, there in enumerate((moved(xyz, axis, 1), moved(xyz, axis, 3))):
            pieces[n].wait_recv()

            def body(i, carry, n=n, there=there):
                at = pl.ds(mult(there[axis] * size + n * cut + i * step, step), step)
                value = src[kind, at, :].astype(jnp.float32) + piece[
                    kind, n, pl.ds(mult(i * step, step), step), :
                ].astype(jnp.float32)
                src[kind, at, :] = value.astype(src.dtype)
                return carry

            lax.fori_loop(0, cut // step, body, 0)
            wholes.append(
                mail.post(
                    src.at[kind, ring_rows(there[axis], size, n * cut, cut), :],
                    whole.at[kind, n, pl.ds(n * cut, cut), :],
                    device_at(there, core),
                )
            )

    down_in = [[], [], []]

    def send_down(step, first, count):
        for g in range(3):
            there = moved(xyz, g, step)
            start = mult(bases[g] + (there[g] * 2 + first) * widths[g], 128)
            down_in[g].append(
                mail.post(
                    down.at[pl.ds(start, count * widths[g]), :],
                    down_land[g].at[step - 1, pl.ds(first * widths[g], count * widths[g]), :],
                    device_at(there, core),
                )
            )

    near_post, far_post = {}, {}
    for kind in range(2):
        for g in range(3):
            for copy in weight_in[kind, g]:
                copy.wait_recv()
            own[kind, g].wait()
            scale_rows((gate_w, up_w)[kind][g], 8 * feat, factors[kind])
            if kind == 0:
                for copy in tok_cross[g]:
                    copy.wait_recv()
                own["tok", g].wait()
            partial_sums(kind, g)
            near_post[kind, g] = send_ring(
                part[g], near[g], half[g], SUM_AXES[g][0], kind, quarter
            )
        if kind == 0:
            send_down(1, 0, 2)
            send_down(3, 0, 2)
    for kind in range(2):
        for g in range(3):
            pass_ring(
                part[g], near[g], half[g], SUM_AXES[g][0], kind, quarter, near_post[kind, g]
            )

    def down_column(g, step, p):
        position = lax.rem(xyz[g] + SIDE - step, SIDE)
        return mult((p * 4 + position) * feat, feat)

    def load_down(g, step):
        for p in range(2):
            if step == 0:
                start = mult(bases[g] + (xyz[g] * 2 + p) * widths[g], 128)
                src = down.at[pl.ds(start, widths[g]), :]
            else:
                src = down_land[g].at[step - 1, pl.ds(p * widths[g], widths[g]), :]
            keep(
                ("down", g, step, p),
                src,
                gate_w[g].at[pl.ds(0, widths[g]), pl.ds(down_column(g, step, p), feat)],
                9 + 8 * g + 2 * step + p,
            )

    def scale_down(g, step):
        for p in range(2):
            own["down", g, step, p].wait()
            scale_block(gate_w[g], widths[g], down_column(g, step, p), feat, factors[2])

    for g in range(3):
        load_down(g, 0)
        for n, step in enumerate((1, 3)):
            down_in[g][n].wait_recv()
            load_down(g, step)
    for g in range(3):
        for step in (0, 1, 3):
            scale_down(g, step)

    for kind in range(2):
        for g in range(3):
            for copy in near_post[kind, g][1]:
                copy.wait_recv()

            def body(i, carry, kind=kind, g=g):
                at = pl.ds(mult(i * 16, 16), 16)
                total[g][kind, at, :] = total[g][kind, at, :] + (
                    near[g][kind, 0, at, :].astype(jnp.float32)
                    + near[g][kind, 1, at, :].astype(jnp.float32)
                )
                return carry

            lax.fori_loop(0, quarter // 16, body, 0)
            far_post[kind, g] = send_ring(
                total[g], far[g], far_half[g], SUM_AXES[g][1], kind, slab
            )
    for kind in range(2):
        for g in range(3):
            pass_ring(
                total[g], far[g], far_half[g], SUM_AXES[g][1], kind, slab, far_post[kind, g]
            )
    send_down(2, 0, 1)

    slab_in = [[], [], []]
    for g in range(3):
        b_axis, c_axis = SUM_AXES[g]
        for kind in range(2):
            for copy in far_post[kind, g][1]:
                copy.wait_recv()
        start = xyz[b_axis] * quarter + xyz[c_axis] * slab

        def body(i, carry, g=g, c_axis=c_axis, start=start):
            at = pl.ds(mult(i * 16, 16), 16)
            mine = pl.ds(mult(xyz[c_axis] * slab + i * 16, 16), 16)
            sums = []
            for kind in range(2):
                value = total[g][kind, mine, :] + (far[g][kind, 0, at, :] + far[g][kind, 1, at, :])
                sums.append(value * units[kind])
            value = sums[0] / (1.0 + jnp.exp(-sums[0])) * sums[1]
            hidden[g][core, pl.ds(mult(start + i * 16, 16), 16), :] = value.astype(jnp.bfloat16)
            return carry

        lax.fori_loop(0, slab // 16, body, 0)
        home = hidden[g].at[core, pl.ds(mult(start, slab), slab), :]
        for step in (2, 1, 3):
            slab_in[g].append(mail.post(home, home, device_at(moved(xyz, c_axis, step), core)))
    send_down(2, 1, 1)

    quarter_in, rest_in, cross_in = [[], [], []], [[], [], []], [[], [], []]

    def hidden_rows(g, step, first, count):
        position = lax.rem(xyz[SUM_AXES[g][0]] + step, SIDE)
        return hidden[g].at[core, ring_rows(position, quarter, first, count), :]

    def cross(g, step):
        view = hidden_rows(g, step, 0, quarter)
        cross_in[g].append(mail.post(view, view, device_at(xyz, other)))

    for g in range(3):
        axis = SUM_AXES[g][0]
        for copy in slab_in[g]:
            copy.wait_recv()
        for first in (0, 1):
            for n, step in enumerate((1, 3)):
                view = hidden_rows(g, 0, mid if first != n else 0, mid)
                quarter_in[g].append(
                    mail.post(view, view, device_at(moved(xyz, axis, step), core))
                )
        cross(g, 0)

    for g in range(3):
        for copy in down_in[g][2:]:
            copy.wait_recv()
        load_down(g, 2)
    mine_out[...] = jnp.zeros_like(mine_out)
    for g in range(3):
        scale_down(g, 2)

    landed_in = {}

    def token_rows(g, step):
        return ring_rows(lax.rem(xyz[SUM_AXES[g][0]] + step, SIDE), quarter, 0, quarter)

    def output_part(g, rows, p):
        return jnp.dot(
            hidden[g][p, rows, :],
            gate_w[g][pl.ds(0, widths[g]), pl.ds(mult(p * 4 * feat, 4 * feat), 4 * feat)],
            preferred_element_type=jnp.float32,
        )

    def output_rows(g, step, value):
        rows = token_rows(g, step)
        for j in range(SIDE):
            block = value[:, j * feat : (j + 1) * feat]
            blocks[j] = block
            sent[g][j, rows, :] = block.astype(jnp.bfloat16)
        mine_out[rows, :] = mine_out[rows, :] + blocks[xyz[g]]
        for move in (2, 1, 3):
            there = moved(xyz, g, move)
            landed_in.setdefault((g, step), []).append(
                mail.post(
                    sent[g].at[there[g], rows, :],
                    landed[g].at[move - 1, rows, :],
                    device_at(there, core),
                )
            )

    def add_landed(g, step):
        for copy in landed_in[g, step]:
            copy.wait_recv()
        rows = token_rows(g, step)
        terms = [landed[g][n, rows, :].astype(jnp.float32) for n in range(3)]
        mine_out[rows, :] = (mine_out[rows, :] + terms[1]) + (terms[0] + terms[2])

    def output_own(step):
        for g in range(3):
            total[g][0, :, pl.ds(0, 4 * feat)] = output_part(g, token_rows(g, step), core)

    def output_rest(n, step):
        for g in range(3):
            cross_in[g][n].wait_recv()
            value = total[g][0, :, pl.ds(0, 4 * feat)] + output_part(g, token_rows(g, step), other)
            output_rows(g, step, value)

    for posts in far_post.values():
        mail.settle(posts[0] + posts[1])
    output_own(0)
    output_rest(0, 0)

    for g in range(3):
        axis = SUM_AXES[g][0]
        for n, (back, on) in enumerate(((3, 1), (1, 3))):
            quarter_in[g][n].wait_recv()
            view = hidden_rows(g, back, n * mid, mid)
            rest_in[g].append(mail.post(view, view, device_at(moved(xyz, axis, on), core)))
    for n, back in enumerate((3, 1)):
        for g in range(3):
            quarter_in[g][2 + n].wait_recv()
            cross(g, back)
    output_own(3)
    output_rest(1, 3)
    output_own(1)
    output_rest(2, 1)
    for g in range(3):
        for copy in rest_in[g]:
            copy.wait_recv()
        cross(g, 2)
    output_own(2)
    for step in (0, 3):
        for g in range(3):
            add_landed(g, step)
    output_rest(3, 2)
    for step in (1, 2):
        for g in range(3):
            add_landed(g, step)
    out[...] = (mine_out[...] * units[2]).astype(jnp.bfloat16)
    mail.finish()


def shards(tokens, gate_weight, up_weight, down_weight):
    toks, feat = tokens.shape
    ff = gate_weight.shape[1]
    widths = class_widths(ff)
    bases = class_bases(widths)
    quarter, slab = toks // 4, toks // 16
    bf16, f32 = jnp.bfloat16, jnp.float32
    hbm = pl.BlockSpec(memory_space=pl.ANY)
    vmem = pl.BlockSpec(memory_space=pltpu.VMEM)
    shape = jax.ShapeDtypeStruct

    scratch = [pltpu.VMEM((max(8 * feat, w), max(8 * feat, w)), bf16) for w in widths]
    scratch += [pltpu.VMEM((8 * feat, w), bf16) for w in widths]
    scratch += [pltpu.VMEM((toks, 8 * feat), bf16) for _ in widths]
    scratch += [pltpu.VMEM((2, toks, w), bf16) for w in widths]
    scratch += [pltpu.VMEM((2, 2, quarter, w), bf16) for w in widths]
    scratch += [pltpu.VMEM((2, 2, quarter // 2, w), bf16) for w in widths]
    scratch += [pltpu.VMEM((2, quarter, w), f32) for w in widths]
    scratch += [pltpu.VMEM((2, 2, slab, w), f32) for w in widths]
    scratch += [pltpu.VMEM((2, 2, slab // 2, w), f32) for w in widths]
    scratch += [pltpu.VMEM((2, toks, w), bf16) for w in widths]
    scratch += [pltpu.VMEM((SIDE, toks, feat), bf16) for _ in widths]
    scratch += [pltpu.VMEM((3, toks, feat), bf16) for _ in widths]
    scratch += [
        pltpu.VMEM((toks, 384), f32),
        pltpu.VMEM((SIDE, quarter, feat), f32),
        pltpu.VMEM((toks, feat), f32),
        pltpu.VMEM((3, 8, 128), f32),
        pltpu.VMEM((13, 8, 128), f32),
        pltpu.SemaphoreType.DMA((238,)),
        pltpu.SemaphoreType.DMA((238,)),
        pltpu.SemaphoreType.DMA((33,)),
        pltpu.SemaphoreType.DMA((100,)),
    ]
    outs = pl.pallas_call(
        functools.partial(kernel, widths, bases),
        out_shape=(
            shape((toks, feat), bf16),
            shape((8, 128), f32),
            *[shape((3, 2 * w, feat), bf16) for w in widths],
        ),
        in_specs=[hbm] * 4,
        out_specs=(vmem, vmem, hbm, hbm, hbm),
        scratch_shapes=scratch,
        compiler_params=pltpu.CompilerParams(
            collective_id=0, has_side_effects=True, vmem_limit_bytes=63 * 2**20
        ),
        name="refit",
    )(tokens, gate_weight, up_weight, down_weight)
    return outs[0], outs[1][:3, 0]


def solution(mesh):
    in_specs = (
        P(None, ("rep", "tp")),
        P(("rep", "tp"), None),
        P(("rep", "tp"), None),
        P(None, ("rep", "tp")),
    )
    out_specs = (P(None, ("rep", "tp")), P())
    return jax.shard_map(shards, mesh=mesh, in_specs=in_specs, out_specs=out_specs, check_vma=False)
```

```python
import functools

import jax
import jax.numpy as jnp
from jax import lax
from jax.experimental import pallas as pl
from jax.experimental.pallas import tpu as pltpu
from jax.sharding import PartitionSpec as P

MESH = pl.DeviceIdType.MESH
SIDE = 4
SUM_AXES = ((1, 2), (2, 0), (0, 1))


def class_widths(ff):
    units = ff // (8 * 128)
    first = (units + 2) // 3
    second = (units - first + 1) // 2
    return [first * 128, second * 128, (units - first - second) * 128]


def class_bases(widths):
    return [0, 8 * widths[0], 8 * (widths[0] + widths[1])]


def place():
    rep = lax.axis_index("rep")
    tp = lax.axis_index("tp")
    return (rep // SIDE, tp // 2, lax.rem(rep, SIDE)), lax.rem(tp, 2)


def device_at(xyz, core):
    return (xyz[0] * SIDE + xyz[2], xyz[1] * 2 + core)


def moved(xyz, axis, step):
    out = list(xyz)
    out[axis] = lax.rem(xyz[axis] + step, SIDE)
    return tuple(out)


def mult(value, of):
    return pl.multiple_of(value, of)


class Mail:
    def __init__(self, send_sems, recv_sems):
        self.send_sems, self.recv_sems, self.used, self.sent = send_sems, recv_sems, 0, []

    def post(self, src, dst, device):
        copy = pltpu.make_async_remote_copy(
            src_ref=src,
            dst_ref=dst,
            send_sem=self.send_sems.at[self.used],
            recv_sem=self.recv_sems.at[self.used],
            device_id=device,
            device_id_type=MESH,
        )
        self.used += 1
        copy.start()
        self.sent.append(copy)
        return copy

    def finish(self):
        for copy in self.sent:
            copy.wait_send()


def greet(partners):
    for partner in partners:
        pl.semaphore_signal(
            pltpu.get_barrier_semaphore(), inc=1, device_id=partner, device_id_type=MESH
        )


def scale_rows(ref, rows, factor, step=32):
    def body(i, carry):
        at = pl.ds(mult(i * step, step), step)
        wide = ref[at, :].astype(jnp.float32)
        ref[at, :] = jnp.floor(wide * factor + 0.5).astype(jnp.bfloat16)
        return carry

    lax.fori_loop(0, rows // step, body, 0)


def scale_block(ref, rows, col, cols, factor, step=64):
    def body(i, carry):
        at = pl.ds(mult(i * step, step), step)
        wide = ref[at, pl.ds(col, cols)].astype(jnp.float32)
        ref[at, pl.ds(col, cols)] = jnp.floor(wide * factor + 0.5).astype(jnp.bfloat16)
        return carry

    lax.fori_loop(0, rows // step, body, 0)


def kernel(widths, bases, tokens, gate, up, down, *refs):
    refs = list(refs)

    def take(n):
        out = refs[:n]
        del refs[:n]
        return out

    out, peaks_out = take(2)
    down_land = take(3)
    gate_w, up_w, tok, part, near, half, kept, total, far, hidden, sent, landed = (
        take(3) for _ in range(12)
    )
    acc, blocks, mine_out, peak_send, peak_recv = take(5)
    send_sems, recv_sems, own_sems, load_sems = take(4)
    toks, feat = tokens.shape
    quarter, slab = toks // 4, toks // 16
    mid = quarter // 2
    xyz, core = place()
    other = 1 - core
    mail = Mail(send_sems, recv_sems)

    partners = [device_at(xyz, other)]
    for axis in range(3):
        for step in range(1, SIDE):
            for c in range(2):
                partners.append(device_at(moved(xyz, axis, step), c))
    greet(partners)

    def load(source, spots, first):
        copies = []
        for g in range(3):
            if source is down:
                pieces = 2 * (widths[g] // feat)
            else:
                pieces = 8
            for p in range(pieces):
                if source is down:
                    rows = 4 * feat
                    start = bases[g] + p * rows
                    view = spots[g].at[
                        p % 2, pl.ds(0, rows), pl.ds((p // 2) * feat, feat)
                    ]
                    origin = source.at[pl.ds(start, rows), :]
                else:
                    view = spots[g].at[p // 4, pl.ds((p % 4) * feat, feat), :]
                    origin = source.at[:, pl.ds(bases[g] + p * widths[g], widths[g])]
                copies.append(
                    pltpu.make_async_copy(origin, view, load_sems.at[first + len(copies)])
                )
        for copy in copies:
            copy.start()
        return copies

    def top_of(spots, copies):
        for copy in copies:
            copy.wait()
        best = None
        for g in range(3):

            def body(i, carry, g=g):
                at = pl.ds(mult(i * 32, 32), 32)
                return jnp.maximum(
                    carry, jnp.maximum(jnp.abs(spots[g][0, at, :]), jnp.abs(spots[g][1, at, :]))
                )

            high = lax.fori_loop(
                0, 4 * feat // 32, body, jnp.zeros((32, widths[g]), jnp.bfloat16)
            )
            high = jnp.max(high.astype(jnp.float32))
            best = high if best is None else jnp.maximum(best, high)
        return best

    gate_load = load(gate, part, 0)

    own = {}

    def keep(name, src, dst, sem):
        copy = pltpu.make_async_copy(src, dst, own_sems.at[sem])
        copy.start()
        own[name] = copy

    def token_spot(g, position, c):
        return tok[g].at[:, pl.ds(mult((position * 2 + c) * feat, feat), feat)]

    def weight_spot(kind, g):
        slot = mult((xyz[g] * 2 + core) * feat, feat)
        return (gate_w, up_w)[kind][g].at[pl.ds(slot, feat), pl.ds(0, widths[g])]

    def weight_part(kind, g, position, c):
        col = mult(bases[g] + (position * 2 + c) * widths[g], 128)
        return (gate, up)[kind].at[:, pl.ds(col, widths[g])]

    pl.semaphore_wait(pltpu.get_barrier_semaphore(), len(partners))

    tok_in, tok_rest, tok_cross = ([[], [], []] for _ in range(3))

    def cross_tokens(g, step):
        spot = token_spot(g, lax.rem(xyz[g] + step, SIDE), core)
        tok_cross[g].append(mail.post(spot, spot, device_at(xyz, other)))

    for step in (1, 3):
        for g in range(3):
            there = device_at(moved(xyz, g, step), core)
            tok_in[g].append(mail.post(tokens, token_spot(g, xyz[g], core), there))
    for g in range(3):
        tok_cross[g].append(
            mail.post(tokens, token_spot(g, xyz[g], core), device_at(xyz, other))
        )

    def pass_tokens(g):
        for n, (back, on) in enumerate(((3, 1), (1, 3))):
            tok_in[g][n].wait_recv()
            slot = mult((lax.rem(xyz[g] + back, SIDE) * 2 + core) * feat, feat)
            view = tok[g].at[pl.ds(n * (toks // 2), toks // 2), pl.ds(slot, feat)]
            tok_rest[g].append(mail.post(view, view, device_at(moved(xyz, g, on), core)))
        cross_tokens(g, 3)
        cross_tokens(g, 1)

    weight_in = {}

    def send_weights(kind, step, flip):
        for g in range(3):
            there = moved(xyz, g, step)
            c = core if flip == 0 else other
            weight_in.setdefault((kind, g), []).append(
                mail.post(
                    weight_part(kind, g, there[g], c), weight_spot(kind, g), device_at(there, c)
                )
            )

    send_weights(0, 1, 0)
    send_weights(0, 3, 0)
    up_load = load(up, hidden, 24)
    for g in range(3):
        keep(("tok", g), tokens, token_spot(g, xyz[g], core), g)
        for kind in range(2):
            keep((kind, g), weight_part(kind, g, xyz[g], core), weight_spot(kind, g), 3 + 2 * g + kind)
    gate_top = top_of(part, gate_load)
    down_load = load(down, part, 48)
    up_top = top_of(hidden, up_load)
    down_top = top_of(part, down_load)
    row = lax.broadcasted_iota(jnp.int32, (8, 128), 0)
    tile = jnp.where(row == 0, gate_top, jnp.where(row == 1, up_top, down_top))

    got = 0
    for axis in range(3):
        peak_send[axis] = tile
        waits = []
        for step in range(SIDE):
            for flip in range(2):
                if step == 0 and flip == 0 or axis > 0 and flip == 1:
                    continue
                there = device_at(moved(xyz, axis, step), core if flip == 0 else other)
                waits.append((got, mail.post(peak_send.at[axis], peak_recv.at[got], there)))
                got += 1
        if axis == 0:
            send_weights(0, 1, 1)
            send_weights(0, 3, 1)
        elif axis == 1:
            for g in range(3):
                pass_tokens(g)
            send_weights(0, 2, 0)
        else:
            send_weights(0, 2, 1)
            send_weights(0, 0, 1)
            for flip in range(2):
                for step in (2, 1, 3):
                    send_weights(1, step, flip)
            send_weights(1, 0, 1)
            for g in range(3):
                for copy in tok_rest[g]:
                    copy.wait_recv()
                cross_tokens(g, 2)
        for n, copy in waits:
            copy.wait_recv()
            tile = jnp.maximum(tile, peak_recv[n])
    peaks_out[...] = tile
    factors = [jnp.max(127.0 / tile[k : k + 1, :]) for k in range(3)]
    units = [jnp.max(tile[k : k + 1, :] / 127.0) for k in range(3)]

    def partial_sums(kind, g):
        width = widths[g]
        cols = 384 if width % 384 == 0 else 256 if width % 256 == 0 else 128
        axis = SUM_AXES[g][0]
        b = xyz[axis]
        neighbours = (moved(xyz, axis, 1)[axis], moved(xyz, axis, 3)[axis])
        weights = (gate_w, up_w)[kind][g]

        def body(j, carry):
            at = pl.ds(mult(j * cols, 128), cols)
            acc[:, pl.ds(0, cols)] = jnp.dot(
                tok[g][...], weights[pl.ds(0, 8 * feat), at], preferred_element_type=jnp.float32
            )
            part[g][kind, :, at] = acc[:, pl.ds(0, cols)].astype(jnp.bfloat16)
            mine = pl.ds(mult(b * quarter, quarter), quarter)
            total[g][kind, :, at] = acc[mine, pl.ds(0, cols)]
            for n in range(2):
                passed = pl.ds(mult(neighbours[n] * quarter + n * mid, mid), mid)
                kept[g][kind, n, :, at] = acc[passed, pl.ds(0, cols)]
            return carry

        lax.fori_loop(0, width // cols, body, 0)

    def ring_rows(position, first, count):
        return pl.ds(mult(position * quarter + first, 16), count)

    def send_near(kind, g):
        axis = SUM_AXES[g][0]
        after, before, far_off = (moved(xyz, axis, s) for s in (1, 3, 2))
        pieces = [
            mail.post(
                part[g].at[kind, ring_rows(far_off[axis], n * mid, mid), :],
                half[g].at[kind, n],
                device_at(there, core),
            )
            for n, there in enumerate((after, before))
        ]
        wholes = [
            mail.post(
                part[g].at[kind, ring_rows(there[axis], (1 - n) * mid, mid), :],
                near[g].at[kind, n, pl.ds((1 - n) * mid, mid), :],
                device_at(there, core),
            )
            for n, there in enumerate((after, before))
        ]
        return pieces, wholes

    def pass_near(kind, g, posts):
        axis = SUM_AXES[g][0]
        pieces, wholes = posts
        for n, there in enumerate((moved(xyz, axis, 1), moved(xyz, axis, 3))):
            pieces[n].wait_recv()

            def body(i, carry, n=n, there=there):
                local = pl.ds(mult(i * 16, 16), 16)
                value = kept[g][kind, n, local, :] + half[g][kind, n, local, :].astype(jnp.float32)
                at = ring_rows(there[axis], n * mid + i * 16, 16)
                part[g][kind, at, :] = value.astype(jnp.bfloat16)
                return carry

            lax.fori_loop(0, mid // 16, body, 0)
            wholes.append(
                mail.post(
                    part[g].at[kind, ring_rows(there[axis], n * mid, mid), :],
                    near[g].at[kind, n, pl.ds(n * mid, mid), :],
                    device_at(there, core),
                )
            )

    down_in = [[], [], []]

    def send_down(step, first, count):
        for g in range(3):
            there = moved(xyz, g, step)
            start = mult(bases[g] + (there[g] * 2 + first) * widths[g], 128)
            down_in[g].append(
                mail.post(
                    down.at[pl.ds(start, count * widths[g]), :],
                    down_land[g].at[step - 1, pl.ds(first * widths[g], count * widths[g]), :],
                    device_at(there, core),
                )
            )

    near_post, far_in = {}, [[], [], []]
    for kind in range(2):
        for g in range(3):
            for copy in weight_in[kind, g]:
                copy.wait_recv()
            own[kind, g].wait()
            scale_rows((gate_w, up_w)[kind][g], 8 * feat, factors[kind])
            if kind == 0:
                for copy in tok_cross[g]:
                    copy.wait_recv()
                own["tok", g].wait()
            partial_sums(kind, g)
            near_post[kind, g] = send_near(kind, g)
        if kind == 0:
            send_down(1, 0, 2)
            send_down(3, 0, 2)
    for kind in range(2):
        for g in range(3):
            pass_near(kind, g, near_post[kind, g])

    def down_column(g, step, p):
        position = lax.rem(xyz[g] + SIDE - step, SIDE)
        return mult((p * 4 + position) * feat, feat)

    def load_down(g, step):
        for p in range(2):
            if step == 0:
                start = mult(bases[g] + (xyz[g] * 2 + p) * widths[g], 128)
                src = down.at[pl.ds(start, widths[g]), :]
            else:
                src = down_land[g].at[step - 1, pl.ds(p * widths[g], widths[g]), :]
            keep(
                ("down", g, step, p),
                src,
                gate_w[g].at[pl.ds(0, widths[g]), pl.ds(down_column(g, step, p), feat)],
                9 + 8 * g + 2 * step + p,
            )

    def scale_down(g, step):
        for p in range(2):
            own["down", g, step, p].wait()
            scale_block(gate_w[g], widths[g], down_column(g, step, p), feat, factors[2])

    for g in range(3):
        load_down(g, 0)
        for n, step in enumerate((1, 3)):
            down_in[g][n].wait_recv()
            load_down(g, step)
    for g in range(3):
        for step in (0, 1, 3):
            scale_down(g, step)

    for kind in range(2):
        for g in range(3):
            for copy in near_post[kind, g][1]:
                copy.wait_recv()

            b_axis, c_axis = SUM_AXES[g]

            def body(i, carry, kind=kind, g=g, b_axis=b_axis):
                at = pl.ds(mult(i * 16, 16), 16)
                value = total[g][kind, at, :] + (
                    near[g][kind, 0, at, :].astype(jnp.float32)
                    + near[g][kind, 1, at, :].astype(jnp.float32)
                )
                total[g][kind, at, :] = value
                part[g][kind, ring_rows(xyz[b_axis], i * 16, 16), :] = value.astype(jnp.bfloat16)
                return carry

            lax.fori_loop(0, quarter // 16, body, 0)
            for step in (2, 1, 3):
                there = moved(xyz, c_axis, step)
                far_in[g].append(
                    mail.post(
                        part[g].at[kind, ring_rows(xyz[b_axis], there[c_axis] * slab, slab), :],
                        far[g].at[kind, step - 1],
                        device_at(there, core),
                    )
                )
    send_down(2, 0, 1)

    slab_in = [[], [], []]
    for g in range(3):
        b_axis, c_axis = SUM_AXES[g]
        for copy in far_in[g]:
            copy.wait_recv()
        start = xyz[b_axis] * quarter + xyz[c_axis] * slab

        def body(i, carry, g=g, c_axis=c_axis, start=start):
            at = pl.ds(mult(i * 16, 16), 16)
            mine = pl.ds(mult(xyz[c_axis] * slab + i * 16, 16), 16)
            sums = []
            for kind in range(2):
                terms = [far[g][kind, n, at, :].astype(jnp.float32) for n in range(3)]
                value = (total[g][kind, mine, :] + terms[1]) + (terms[0] + terms[2])
                sums.append(value * units[kind])
            value = sums[0] / (1.0 + jnp.exp(-sums[0])) * sums[1]
            hidden[g][core, pl.ds(mult(start + i * 16, 16), 16), :] = value.astype(jnp.bfloat16)
            return carry

        lax.fori_loop(0, slab // 16, body, 0)
        home = hidden[g].at[core, pl.ds(mult(start, slab), slab), :]
        for step in (2, 1, 3):
            slab_in[g].append(mail.post(home, home, device_at(moved(xyz, c_axis, step), core)))
    send_down(2, 1, 1)

    quarter_in, rest_in, cross_in = [[], [], []], [[], [], []], [[], [], []]

    def hidden_rows(g, step, first, count):
        position = lax.rem(xyz[SUM_AXES[g][0]] + step, SIDE)
        return hidden[g].at[core, ring_rows(position, first, count), :]

    def cross(g, step):
        view = hidden_rows(g, step, 0, quarter)
        cross_in[g].append(mail.post(view, view, device_at(xyz, other)))

    for g in range(3):
        axis = SUM_AXES[g][0]
        for copy in slab_in[g]:
            copy.wait_recv()
        for first in (0, 1):
            for n, step in enumerate((1, 3)):
                view = hidden_rows(g, 0, mid if first != n else 0, mid)
                quarter_in[g].append(
                    mail.post(view, view, device_at(moved(xyz, axis, step), core))
                )
        cross(g, 0)

    for g in range(3):
        for copy in down_in[g][2:]:
            copy.wait_recv()
        load_down(g, 2)
    mine_out[...] = jnp.zeros_like(mine_out)
    for g in range(3):
        scale_down(g, 2)

    landed_in = {}

    def token_rows(g, step):
        return ring_rows(lax.rem(xyz[SUM_AXES[g][0]] + step, SIDE), 0, quarter)

    def output_part(g, rows, p):
        return jnp.dot(
            hidden[g][p, rows, :],
            gate_w[g][pl.ds(0, widths[g]), pl.ds(mult(p * 4 * feat, 4 * feat), 4 * feat)],
            preferred_element_type=jnp.float32,
        )

    def output_rows(g, step, value):
        rows = token_rows(g, step)
        for j in range(SIDE):
            block = value[:, j * feat : (j + 1) * feat]
            blocks[j] = block
            sent[g][j, rows, :] = block.astype(jnp.bfloat16)
        mine_out[rows, :] = mine_out[rows, :] + blocks[xyz[g]]
        for move in (2, 1, 3):
            there = moved(xyz, g, move)
            landed_in.setdefault((g, step), []).append(
                mail.post(
                    sent[g].at[there[g], rows, :],
                    landed[g].at[move - 1, rows, :],
                    device_at(there, core),
                )
            )

    def add_landed(g, step):
        for copy in landed_in[g, step]:
            copy.wait_recv()
        rows = token_rows(g, step)
        terms = [landed[g][n, rows, :].astype(jnp.float32) for n in range(3)]
        mine_out[rows, :] = (mine_out[rows, :] + terms[1]) + (terms[0] + terms[2])

    def output_own(step):
        for g in range(3):
            total[g][0, :, pl.ds(0, 4 * feat)] = output_part(g, token_rows(g, step), core)

    def output_rest(n, step):
        for g in range(3):
            cross_in[g][n].wait_recv()
            value = total[g][0, :, pl.ds(0, 4 * feat)] + output_part(g, token_rows(g, step), other)
            output_rows(g, step, value)

    output_own(0)
    output_rest(0, 0)

    for g in range(3):
        axis = SUM_AXES[g][0]
        for n, (back, on) in enumerate(((3, 1), (1, 3))):
            quarter_in[g][n].wait_recv()
            view = hidden_rows(g, back, n * mid, mid)
            rest_in[g].append(mail.post(view, view, device_at(moved(xyz, axis, on), core)))
    for n, back in enumerate((3, 1)):
        for g in range(3):
            quarter_in[g][2 + n].wait_recv()
            cross(g, back)
    output_own(3)
    output_rest(1, 3)
    output_own(1)
    output_rest(2, 1)
    for g in range(3):
        for copy in rest_in[g]:
            copy.wait_recv()
        cross(g, 2)
    output_own(2)
    for step in (0, 3):
        for g in range(3):
            add_landed(g, step)
    output_rest(3, 2)
    for step in (1, 2):
        for g in range(3):
            add_landed(g, step)
    out[...] = (mine_out[...] * units[2]).astype(jnp.bfloat16)
    mail.finish()


def shards(tokens, gate_weight, up_weight, down_weight):
    toks, feat = tokens.shape
    ff = gate_weight.shape[1]
    widths = class_widths(ff)
    bases = class_bases(widths)
    quarter, slab = toks // 4, toks // 16
    bf16, f32 = jnp.bfloat16, jnp.float32
    hbm = pl.BlockSpec(memory_space=pl.ANY)
    vmem = pl.BlockSpec(memory_space=pltpu.VMEM)
    shape = jax.ShapeDtypeStruct

    scratch = [pltpu.VMEM((max(8 * feat, w), max(8 * feat, w)), bf16) for w in widths]
    scratch += [pltpu.VMEM((8 * feat, w), bf16) for w in widths]
    scratch += [pltpu.VMEM((toks, 8 * feat), bf16) for _ in widths]
    scratch += [pltpu.VMEM((2, toks, w), bf16) for w in widths]
    scratch += [pltpu.VMEM((2, 2, quarter, w), bf16) for w in widths]
    scratch += [pltpu.VMEM((2, 2, quarter // 2, w), bf16) for w in widths]
    scratch += [pltpu.VMEM((2, 2, quarter // 2, w), f32) for w in widths]
    scratch += [pltpu.VMEM((2, quarter, w), f32) for w in widths]
    scratch += [pltpu.VMEM((2, 3, slab, w), bf16) for w in widths]
    scratch += [pltpu.VMEM((2, toks, w), bf16) for w in widths]
    scratch += [pltpu.VMEM((SIDE, toks, feat), bf16) for _ in widths]
    scratch += [pltpu.VMEM((3, toks, feat), bf16) for _ in widths]
    scratch += [
        pltpu.VMEM((toks, 384), f32),
        pltpu.VMEM((SIDE, quarter, feat), f32),
        pltpu.VMEM((toks, feat), f32),
        pltpu.VMEM((3, 8, 128), f32),
        pltpu.VMEM((13, 8, 128), f32),
        pltpu.SemaphoreType.DMA((220,)),
        pltpu.SemaphoreType.DMA((220,)),
        pltpu.SemaphoreType.DMA((33,)),
        pltpu.SemaphoreType.DMA((100,)),
    ]
    outs = pl.pallas_call(
        functools.partial(kernel, widths, bases),
        out_shape=(
            shape((toks, feat), bf16),
            shape((8, 128), f32),
            *[shape((3, 2 * w, feat), bf16) for w in widths],
        ),
        in_specs=[hbm] * 4,
        out_specs=(vmem, vmem, hbm, hbm, hbm),
        scratch_shapes=scratch,
        compiler_params=pltpu.CompilerParams(
            collective_id=0, has_side_effects=True, vmem_limit_bytes=63 * 2**20
        ),
        name="refit",
    )(tokens, gate_weight, up_weight, down_weight)
    return outs[0], outs[1][:3, 0]


def solution(mesh):
    in_specs = (
        P(None, ("rep", "tp")),
        P(("rep", "tp"), None),
        P(("rep", "tp"), None),
        P(None, ("rep", "tp")),
    )
    out_specs = (P(None, ("rep", "tp")), P())
    return jax.shard_map(shards, mesh=mesh, in_specs=in_specs, out_specs=out_specs, check_vma=False)
```

```python
import functools

import jax
import jax.numpy as jnp
from jax import lax
from jax.experimental import pallas as pl
from jax.experimental.pallas import tpu as pltpu
from jax.sharding import PartitionSpec as P

MESH = pl.DeviceIdType.MESH
SIDE = 4
SUM_AXES = ((1, 2), (2, 0), (0, 1))


def class_widths(ff):
    units = ff // (8 * 128)
    first = (units + 2) // 3
    second = (units - first + 1) // 2
    return [first * 128, second * 128, (units - first - second) * 128]


def class_bases(widths):
    return [0, 8 * widths[0], 8 * (widths[0] + widths[1])]


def place():
    rep = lax.axis_index("rep")
    tp = lax.axis_index("tp")
    return (rep // SIDE, tp // 2, lax.rem(rep, SIDE)), lax.rem(tp, 2)


def device_at(xyz, core):
    return (xyz[0] * SIDE + xyz[2], xyz[1] * 2 + core)


def moved(xyz, axis, step):
    out = list(xyz)
    out[axis] = lax.rem(xyz[axis] + step, SIDE)
    return tuple(out)


def mult(value, of):
    return pl.multiple_of(value, of)


class Mail:
    def __init__(self, send_sems, recv_sems):
        self.send_sems, self.recv_sems, self.used, self.sent = send_sems, recv_sems, 0, []

    def post(self, src, dst, device):
        copy = pltpu.make_async_remote_copy(
            src_ref=src,
            dst_ref=dst,
            send_sem=self.send_sems.at[self.used],
            recv_sem=self.recv_sems.at[self.used],
            device_id=device,
            device_id_type=MESH,
        )
        self.used += 1
        copy.start()
        self.sent.append(copy)
        return copy

    def finish(self, count=None):
        done = self.sent[:count]
        self.sent = self.sent[len(done) :]
        for copy in done:
            copy.wait_send()


def greet(partners):
    for partner in partners:
        pl.semaphore_signal(
            pltpu.get_barrier_semaphore(), inc=1, device_id=partner, device_id_type=MESH
        )


def scale_rows(ref, rows, factor, step=32):
    def body(i, carry):
        at = pl.ds(mult(i * step, step), step)
        wide = ref[at, :].astype(jnp.float32)
        ref[at, :] = jnp.floor(wide * factor + 0.5).astype(jnp.bfloat16)
        return carry

    lax.fori_loop(0, rows // step, body, 0)


def scale_block(ref, rows, col, cols, factor, step=64):
    def body(i, carry):
        at = pl.ds(mult(i * step, step), step)
        wide = ref[at, pl.ds(col, cols)].astype(jnp.float32)
        ref[at, pl.ds(col, cols)] = jnp.floor(wide * factor + 0.5).astype(jnp.bfloat16)
        return carry

    lax.fori_loop(0, rows // step, body, 0)


def kernel(widths, bases, tokens, gate, up, down, *refs):
    refs = list(refs)

    def take(n):
        out = refs[:n]
        del refs[:n]
        return out

    out, peaks_out = take(2)
    down_land = take(3)
    gate_w, up_w, tok, part, near, half, kept, total, far, hidden, sent, landed = (
        take(3) for _ in range(12)
    )
    acc, blocks, mine_out, peak_send, peak_recv = take(5)
    send_sems, recv_sems, own_sems, load_sems = take(4)
    toks, feat = tokens.shape
    quarter, slab = toks // 4, toks // 16
    mid = quarter // 2
    xyz, core = place()
    other = 1 - core
    mail = Mail(send_sems, recv_sems)

    partners = [device_at(xyz, other)]
    for axis in range(3):
        for step in range(1, SIDE):
            for c in range(2):
                partners.append(device_at(moved(xyz, axis, step), c))
    greet(partners)

    def load(source, spots, first):
        copies = []
        for g in range(3):
            if source is down:
                pieces = 2 * (widths[g] // feat)
            else:
                pieces = 8
            for p in range(pieces):
                if source is down:
                    rows = 4 * feat
                    start = bases[g] + p * rows
                    view = spots[g].at[
                        p % 2, pl.ds(0, rows), pl.ds((p // 2) * feat, feat)
                    ]
                    origin = source.at[pl.ds(start, rows), :]
                else:
                    view = spots[g].at[p // 4, pl.ds((p % 4) * feat, feat), :]
                    origin = source.at[:, pl.ds(bases[g] + p * widths[g], widths[g])]
                copies.append(
                    pltpu.make_async_copy(origin, view, load_sems.at[first + len(copies)])
                )
        for copy in copies:
            copy.start()
        return copies

    def top_of(spots, copies):
        for copy in copies:
            copy.wait()
        best = None
        for g in range(3):

            def body(i, carry, g=g):
                at = pl.ds(mult(i * 32, 32), 32)
                return jnp.maximum(
                    carry, jnp.maximum(jnp.abs(spots[g][0, at, :]), jnp.abs(spots[g][1, at, :]))
                )

            high = lax.fori_loop(
                0, 4 * feat // 32, body, jnp.zeros((32, widths[g]), jnp.bfloat16)
            )
            high = jnp.max(high.astype(jnp.float32))
            best = high if best is None else jnp.maximum(best, high)
        return best

    gate_load = load(gate, part, 0)

    own = {}

    def keep(name, src, dst, sem):
        copy = pltpu.make_async_copy(src, dst, own_sems.at[sem])
        copy.start()
        own[name] = copy

    def token_spot(g, position, c):
        return tok[g].at[:, pl.ds(mult((position * 2 + c) * feat, feat), feat)]

    def weight_spot(kind, g):
        slot = mult((xyz[g] * 2 + core) * feat, feat)
        return (gate_w, up_w)[kind][g].at[pl.ds(slot, feat), pl.ds(0, widths[g])]

    def weight_part(kind, g, position, c):
        col = mult(bases[g] + (position * 2 + c) * widths[g], 128)
        return (gate, up)[kind].at[:, pl.ds(col, widths[g])]

    pl.semaphore_wait(pltpu.get_barrier_semaphore(), len(partners))

    tok_in, tok_rest, tok_cross = ([[], [], []] for _ in range(3))

    def cross_tokens(g, step):
        spot = token_spot(g, lax.rem(xyz[g] + step, SIDE), core)
        tok_cross[g].append(mail.post(spot, spot, device_at(xyz, other)))

    for step in (1, 3):
        for g in range(3):
            there = device_at(moved(xyz, g, step), core)
            tok_in[g].append(mail.post(tokens, token_spot(g, xyz[g], core), there))
    for g in range(3):
        tok_cross[g].append(
            mail.post(tokens, token_spot(g, xyz[g], core), device_at(xyz, other))
        )

    def pass_tokens(g):
        for n, (back, on) in enumerate(((3, 1), (1, 3))):
            tok_in[g][n].wait_recv()
            slot = mult((lax.rem(xyz[g] + back, SIDE) * 2 + core) * feat, feat)
            view = tok[g].at[pl.ds(n * (toks // 2), toks // 2), pl.ds(slot, feat)]
            tok_rest[g].append(mail.post(view, view, device_at(moved(xyz, g, on), core)))
        cross_tokens(g, 3)
        cross_tokens(g, 1)

    weight_in = {}

    def send_weights(kind, step, flip):
        for g in range(3):
            there = moved(xyz, g, step)
            c = core if flip == 0 else other
            weight_in.setdefault((kind, g), []).append(
                mail.post(
                    weight_part(kind, g, there[g], c), weight_spot(kind, g), device_at(there, c)
                )
            )

    send_weights(0, 1, 0)
    send_weights(0, 3, 0)
    send_weights(0, 1, 1)
    send_weights(0, 3, 1)
    up_load = load(up, hidden, 24)
    for g in range(3):
        keep(("tok", g), tokens, token_spot(g, xyz[g], core), g)
        for kind in range(2):
            keep((kind, g), weight_part(kind, g, xyz[g], core), weight_spot(kind, g), 3 + 2 * g + kind)
    gate_top = top_of(part, gate_load)
    down_load = load(down, part, 48)
    up_top = top_of(hidden, up_load)
    down_top = top_of(part, down_load)
    row = lax.broadcasted_iota(jnp.int32, (8, 128), 0)
    tile = jnp.where(row == 0, gate_top, jnp.where(row == 1, up_top, down_top))

    got = 0
    for axis in range(3):
        peak_send[axis] = tile
        waits = []
        for step in range(SIDE):
            for flip in range(2):
                if step == 0 and flip == 0 or axis > 0 and flip == 1:
                    continue
                there = device_at(moved(xyz, axis, step), core if flip == 0 else other)
                waits.append((got, mail.post(peak_send.at[axis], peak_recv.at[got], there)))
                got += 1
        if axis == 0:
            send_weights(0, 2, 0)
        elif axis == 1:
            for g in range(3):
                pass_tokens(g)
            send_weights(0, 2, 1)
        else:
            send_weights(0, 0, 1)
            for step in (1, 3):
                for flip in range(2):
                    send_weights(1, step, flip)
            for flip in range(2):
                send_weights(1, 2, flip)
            send_weights(1, 0, 1)
            for g in range(3):
                for copy in tok_rest[g]:
                    copy.wait_recv()
                cross_tokens(g, 2)
        for n, copy in waits:
            copy.wait_recv()
            tile = jnp.maximum(tile, peak_recv[n])
    for k in range(3):
        peaks_out[k] = jnp.max(tile[k : k + 1, :])
    factors = [jnp.max(127.0 / tile[k : k + 1, :]) for k in range(3)]
    units = [jnp.max(tile[k : k + 1, :] / 127.0) for k in range(3)]

    def partial_sums(kind, g):
        width = widths[g]
        cols = 384 if width % 384 == 0 else 256 if width % 256 == 0 else 128
        axis = SUM_AXES[g][0]
        b = xyz[axis]
        neighbours = (moved(xyz, axis, 1)[axis], moved(xyz, axis, 3)[axis])
        weights = (gate_w, up_w)[kind][g]

        def body(j, carry):
            at = pl.ds(mult(j * cols, 128), cols)
            acc[:, pl.ds(0, cols)] = jnp.dot(
                tok[g][...], weights[pl.ds(0, 8 * feat), at], preferred_element_type=jnp.float32
            )
            part[g][kind, :, at] = acc[:, pl.ds(0, cols)].astype(jnp.bfloat16)
            mine = pl.ds(mult(b * quarter, quarter), quarter)
            total[g][kind, :, at] = acc[mine, pl.ds(0, cols)]
            for n in range(2):
                passed = pl.ds(mult(neighbours[n] * quarter + n * mid, mid), mid)
                kept[g][kind, n, :, at] = acc[passed, pl.ds(0, cols)]
            return carry

        lax.fori_loop(0, width // cols, body, 0)

    def ring_rows(position, first, count):
        return pl.ds(mult(position * quarter + first, 16), count)

    def send_near(kind, g):
        axis = SUM_AXES[g][0]
        after, before, far_off = (moved(xyz, axis, s) for s in (1, 3, 2))
        pieces = [
            mail.post(
                part[g].at[kind, ring_rows(far_off[axis], n * mid, mid), :],
                half[g].at[kind, n],
                device_at(there, core),
            )
            for n, there in enumerate((after, before))
        ]
        wholes = [
            mail.post(
                part[g].at[kind, ring_rows(there[axis], (1 - n) * mid, mid), :],
                near[g].at[kind, n, pl.ds((1 - n) * mid, mid), :],
                device_at(there, core),
            )
            for n, there in enumerate((after, before))
        ]
        return pieces, wholes

    def pass_near(kind, g, posts):
        axis = SUM_AXES[g][0]
        pieces, wholes = posts
        for n, there in enumerate((moved(xyz, axis, 1), moved(xyz, axis, 3))):
            pieces[n].wait_recv()

            def body(i, carry, n=n, there=there):
                local = pl.ds(mult(i * 16, 16), 16)
                value = kept[g][kind, n, local, :] + half[g][kind, n, local, :].astype(jnp.float32)
                at = ring_rows(there[axis], n * mid + i * 16, 16)
                part[g][kind, at, :] = value.astype(jnp.bfloat16)
                return carry

            lax.fori_loop(0, mid // 16, body, 0)
            wholes.append(
                mail.post(
                    part[g].at[kind, ring_rows(there[axis], n * mid, mid), :],
                    near[g].at[kind, n, pl.ds(n * mid, mid), :],
                    device_at(there, core),
                )
            )

    down_in = [[], [], []]

    def send_down(step, first, count):
        for g in range(3):
            there = moved(xyz, g, step)
            start = mult(bases[g] + (there[g] * 2 + first) * widths[g], 128)
            down_in[g].append(
                mail.post(
                    down.at[pl.ds(start, count * widths[g]), :],
                    down_land[g].at[step - 1, pl.ds(first * widths[g], count * widths[g]), :],
                    device_at(there, core),
                )
            )

    near_post, far_in = {}, [[], [], []]
    for kind in range(2):
        for g in range(3):
            for copy in weight_in[kind, g]:
                copy.wait_recv()
            own[kind, g].wait()
            scale_rows((gate_w, up_w)[kind][g], 8 * feat, factors[kind])
            if kind == 0:
                for copy in tok_cross[g]:
                    copy.wait_recv()
                own["tok", g].wait()
            partial_sums(kind, g)
            near_post[kind, g] = send_near(kind, g)
        if kind == 0:
            send_down(1, 0, 2)
            send_down(3, 0, 2)
    for kind in range(2):
        for g in range(3):
            pass_near(kind, g, near_post[kind, g])
    posted = len(mail.sent)

    def down_column(g, step, p):
        position = lax.rem(xyz[g] + SIDE - step, SIDE)
        return mult((p * 4 + position) * feat, feat)

    def load_down(g, step):
        for p in range(2):
            if step == 0:
                start = mult(bases[g] + (xyz[g] * 2 + p) * widths[g], 128)
                src = down.at[pl.ds(start, widths[g]), :]
            else:
                src = down_land[g].at[step - 1, pl.ds(p * widths[g], widths[g]), :]
            keep(
                ("down", g, step, p),
                src,
                gate_w[g].at[pl.ds(0, widths[g]), pl.ds(down_column(g, step, p), feat)],
                9 + 8 * g + 2 * step + p,
            )

    def scale_down(g, step):
        for p in range(2):
            own["down", g, step, p].wait()
            scale_block(gate_w[g], widths[g], down_column(g, step, p), feat, factors[2])

    for g in range(3):
        load_down(g, 0)
        for n, step in enumerate((1, 3)):
            down_in[g][n].wait_recv()
            load_down(g, step)
    for g in range(3):
        for step in (0, 1, 3):
            scale_down(g, step)

    for kind in range(2):
        for g in range(3):
            for copy in near_post[kind, g][1]:
                copy.wait_recv()

            b_axis, c_axis = SUM_AXES[g]

            def body(i, carry, kind=kind, g=g, b_axis=b_axis):
                at = pl.ds(mult(i * 16, 16), 16)
                value = total[g][kind, at, :] + (
                    near[g][kind, 0, at, :].astype(jnp.float32)
                    + near[g][kind, 1, at, :].astype(jnp.float32)
                )
                total[g][kind, at, :] = value
                part[g][kind, ring_rows(xyz[b_axis], i * 16, 16), :] = value.astype(jnp.bfloat16)
                return carry

            lax.fori_loop(0, quarter // 16, body, 0)
            for step in (2, 1, 3):
                there = moved(xyz, c_axis, step)
                far_in[g].append(
                    mail.post(
                        part[g].at[kind, ring_rows(xyz[b_axis], there[c_axis] * slab, slab), :],
                        far[g].at[kind, step - 1],
                        device_at(there, core),
                    )
                )
    send_down(2, 0, 1)

    slab_in = [[], [], []]
    for g in range(3):
        b_axis, c_axis = SUM_AXES[g]
        for copy in far_in[g]:
            copy.wait_recv()
        start = xyz[b_axis] * quarter + xyz[c_axis] * slab

        def body(i, carry, g=g, c_axis=c_axis, start=start):
            at = pl.ds(mult(i * 16, 16), 16)
            mine = pl.ds(mult(xyz[c_axis] * slab + i * 16, 16), 16)
            sums = []
            for kind in range(2):
                terms = [far[g][kind, n, at, :].astype(jnp.float32) for n in range(3)]
                value = (total[g][kind, mine, :] + terms[1]) + (terms[0] + terms[2])
                sums.append(value * units[kind])
            value = sums[0] / (1.0 + jnp.exp(-sums[0])) * sums[1]
            hidden[g][core, pl.ds(mult(start + i * 16, 16), 16), :] = value.astype(jnp.bfloat16)
            return carry

        lax.fori_loop(0, slab // 16, body, 0)
        home = hidden[g].at[core, pl.ds(mult(start, slab), slab), :]
        for step in (2, 1, 3):
            slab_in[g].append(mail.post(home, home, device_at(moved(xyz, c_axis, step), core)))
    send_down(2, 1, 1)

    quarter_in, rest_in, cross_in = [[], [], []], [[], [], []], [[], [], []]

    def hidden_rows(g, step, first, count):
        position = lax.rem(xyz[SUM_AXES[g][0]] + step, SIDE)
        return hidden[g].at[core, ring_rows(position, first, count), :]

    def cross(g, step):
        view = hidden_rows(g, step, 0, quarter)
        cross_in[g].append(mail.post(view, view, device_at(xyz, other)))

    mail.finish(posted)
    posted = len(mail.sent)

    for g in range(3):
        axis = SUM_AXES[g][0]
        for copy in slab_in[g]:
            copy.wait_recv()
        for first in (0, 1):
            for n, step in enumerate((1, 3)):
                view = hidden_rows(g, 0, mid if first != n else 0, mid)
                quarter_in[g].append(
                    mail.post(view, view, device_at(moved(xyz, axis, step), core))
                )
        cross(g, 0)

    for g in range(3):
        for copy in down_in[g][2:]:
            copy.wait_recv()
        load_down(g, 2)
    mine_out[...] = jnp.zeros_like(mine_out)
    for g in range(3):
        scale_down(g, 2)

    landed_in = {}

    def token_rows(g, step):
        return ring_rows(lax.rem(xyz[SUM_AXES[g][0]] + step, SIDE), 0, quarter)

    def output_part(g, rows, p):
        return jnp.dot(
            hidden[g][p, rows, :],
            gate_w[g][pl.ds(0, widths[g]), pl.ds(mult(p * 4 * feat, 4 * feat), 4 * feat)],
            preferred_element_type=jnp.float32,
        )

    def output_rows(g, step, value):
        rows = token_rows(g, step)
        for j in range(SIDE):
            block = value[:, j * feat : (j + 1) * feat]
            blocks[j] = block
            sent[g][j, rows, :] = block.astype(jnp.bfloat16)
        mine_out[rows, :] = mine_out[rows, :] + blocks[xyz[g]]
        for move in (2, 1, 3):
            there = moved(xyz, g, move)
            landed_in.setdefault((g, step), []).append(
                mail.post(
                    sent[g].at[there[g], rows, :],
                    landed[g].at[move - 1, rows, :],
                    device_at(there, core),
                )
            )

    def add_landed(g, step):
        for copy in landed_in[g, step]:
            copy.wait_recv()
        rows = token_rows(g, step)
        terms = [landed[g][n, rows, :].astype(jnp.float32) for n in range(3)]
        mine_out[rows, :] = (mine_out[rows, :] + terms[1]) + (terms[0] + terms[2])

    def output_own(step):
        for g in range(3):
            total[g][0, :, pl.ds(0, 4 * feat)] = output_part(g, token_rows(g, step), core)

    def output_rest(n, step):
        for g in range(3):
            cross_in[g][n].wait_recv()
            value = total[g][0, :, pl.ds(0, 4 * feat)] + output_part(g, token_rows(g, step), other)
            output_rows(g, step, value)

    output_own(0)
    output_rest(0, 0)

    for g in range(3):
        axis = SUM_AXES[g][0]
        for n, (back, on) in enumerate(((3, 1), (1, 3))):
            quarter_in[g][n].wait_recv()
            view = hidden_rows(g, back, n * mid, mid)
            rest_in[g].append(mail.post(view, view, device_at(moved(xyz, axis, on), core)))
    mail.finish(posted)
    for n, back in enumerate((3, 1)):
        for g in range(3):
            quarter_in[g][2 + n].wait_recv()
            cross(g, back)
    output_own(3)
    output_rest(1, 3)
    output_own(1)
    output_rest(2, 1)
    for g in range(3):
        for copy in rest_in[g]:
            copy.wait_recv()
        cross(g, 2)
    output_own(2)
    for step in (0, 3):
        for g in range(3):
            add_landed(g, step)
    output_rest(3, 2)
    for step in (1, 2):
        for g in range(3):
            add_landed(g, step)
    out[...] = (mine_out[...] * units[2]).astype(jnp.bfloat16)
    mail.finish()


def shards(tokens, gate_weight, up_weight, down_weight):
    toks, feat = tokens.shape
    ff = gate_weight.shape[1]
    widths = class_widths(ff)
    bases = class_bases(widths)
    quarter, slab = toks // 4, toks // 16
    bf16, f32 = jnp.bfloat16, jnp.float32
    hbm = pl.BlockSpec(memory_space=pl.ANY)
    vmem = pl.BlockSpec(memory_space=pltpu.VMEM)
    shape = jax.ShapeDtypeStruct

    scratch = [pltpu.VMEM((max(8 * feat, w), max(8 * feat, w)), bf16) for w in widths]
    scratch += [pltpu.VMEM((8 * feat, w), bf16) for w in widths]
    scratch += [pltpu.VMEM((toks, 8 * feat), bf16) for _ in widths]
    scratch += [pltpu.VMEM((2, toks, w), bf16) for w in widths]
    scratch += [pltpu.VMEM((2, 2, quarter, w), bf16) for w in widths]
    scratch += [pltpu.VMEM((2, 2, quarter // 2, w), bf16) for w in widths]
    scratch += [pltpu.VMEM((2, 2, quarter // 2, w), f32) for w in widths]
    scratch += [pltpu.VMEM((2, quarter, w), f32) for w in widths]
    scratch += [pltpu.VMEM((2, 3, slab, w), bf16) for w in widths]
    scratch += [pltpu.VMEM((2, toks, w), bf16) for w in widths]
    scratch += [pltpu.VMEM((SIDE, toks, feat), bf16) for _ in widths]
    scratch += [pltpu.VMEM((3, toks, feat), bf16) for _ in widths]
    scratch += [
        pltpu.VMEM((toks, 384), f32),
        pltpu.VMEM((SIDE, quarter, feat), f32),
        pltpu.VMEM((toks, feat), f32),
        pltpu.VMEM((3, 8, 128), f32),
        pltpu.VMEM((13, 8, 128), f32),
        pltpu.SemaphoreType.DMA((220,)),
        pltpu.SemaphoreType.DMA((220,)),
        pltpu.SemaphoreType.DMA((33,)),
        pltpu.SemaphoreType.DMA((100,)),
    ]
    outs = pl.pallas_call(
        functools.partial(kernel, widths, bases),
        out_shape=(
            shape((toks, feat), bf16),
            shape((3,), f32),
            *[shape((3, 2 * w, feat), bf16) for w in widths],
        ),
        in_specs=[hbm] * 4,
        out_specs=(vmem, pl.BlockSpec(memory_space=pltpu.SMEM), hbm, hbm, hbm),
        scratch_shapes=scratch,
        compiler_params=pltpu.CompilerParams(
            collective_id=0, has_side_effects=True, vmem_limit_bytes=63 * 2**20
        ),
        name="refit",
    )(tokens, gate_weight, up_weight, down_weight)
    return outs[0], outs[1]


def solution(mesh):
    in_specs = (
        P(None, ("rep", "tp")),
        P(("rep", "tp"), None),
        P(("rep", "tp"), None),
        P(None, ("rep", "tp")),
    )
    out_specs = (P(None, ("rep", "tp")), P())
    return jax.shard_map(shards, mesh=mesh, in_specs=in_specs, out_specs=out_specs, check_vma=False)
```
